128 devices in a mesh: front: 8 (over y, core), grp: 16 (over x, z).
Axes of the slice: x: 4, y: 4, z: 4, core: 2. Of those that a mesh axis runs over, the one named last changes fastest.
Arguments:
- front_entries: bfloat16 [8, 8192, 8192], P('front', 'grp'), may hold values from -6 to 6
- child_blocks: bfloat16 [16384, 32, 512], P(('front', 'grp')), may hold values from -6 to 6
- dest_device: int32 [16384, 1], P(('front', 'grp')), may hold values from 0 to 127; in each aligned block of 128 rows (0 to 127, 128 to 255, ...) at most 2 rows name the same one
- dest_tile: int32 [16384], P(('front', 'grp')), may hold values from 0 to 255
- child_count: int32 [128], P(('front', 'grp')), may hold values from 96 to 128, as said below
- diag_inverse: float32 [8, 2, 512, 512], P('front'), as said below
Outputs:
- schur: bfloat16 [8, 7168, 7168], P('front', 'grp')
- panel_factor: float32 [8, 2, 8192, 512], P('front', None, 'grp')
The draws below stay inside these ranges and needn't reach their ends.
Inputs may be any that keep to these rules, and one draw needn't show every extreme that they name: `dest_device`: the 128 slots of one device name one device at most 2 times, and some device exactly 2 times. `child_count`: some device has all 128 slots live in every draw. `diag_inverse`: each panel's matrix is lower triangular with a positive diagonal.
All inputs are finite; a program needn't handle non-finite values.
Results may differ from the reference program's by a relative error of at most 0.001.
Values may be sent and summed in bfloat16 or wider, within the bound.
No kernel may reach another device: no remote copies, remote signals or barrier semaphores. Data moves between devices by JAX's collectives and lax.ppermute only.
A program may use at most 256 MiB of HBM per device.

```python
import math
import jax
import jax.numpy as jnp
import numpy as np
from jax import lax

F = 8192
PANEL = 512
PANELS = 2
BR = 32
BC = 512
K_DEV = 128
CAP = 2
FRONTS = 8
ROWS_DEV = 512
PIV_DEV = 32
TRAIL = 7168
TILES_DEV = 256
CHILDREN = 16384
N_GRP = 16
DEVICES = 128


def draw_child_count(key, part):
    key = jax.random.fold_in(key, 11)
    device_total = CHILDREN // K_DEV
    first_key, second_key = jax.random.split(key)
    counts = jax.random.randint(first_key, (device_total,), 3 * K_DEV // 4, K_DEV + 1)
    fullest = jax.random.randint(second_key, (), 0, device_total)
    return jnp.where(jnp.arange(device_total) == fullest, K_DEV, counts).astype(jnp.int32)


def draw_diag_inverse(key, part):
    key = jax.random.fold_in(key, 23)
    first_key, second_key = jax.random.split(key)
    diagonal = jax.random.uniform(first_key, (FRONTS, PANELS, PANEL), jnp.float32, 1.0, 2.0)
    spread_part = jax.random.normal(second_key, (FRONTS, PANELS, PANEL, PANEL), jnp.float32) * (0.5 / math.sqrt(PANEL))
    rows_index = jnp.arange(PANEL)[:, None]
    cols_index = jnp.arange(PANEL)[None, :]
    below_diag = rows_index > cols_index
    on_diag = rows_index == cols_index
    matrix = jnp.where(below_diag[None, None], spread_part, 0.0) + jnp.where(on_diag[None, None], diagonal[:, :, :, None], 0.0)
    return (matrix * (2.0 / math.sqrt(PANEL))).astype(jnp.float32)


def set_ends(values, stream_key, least, top_value):
    spot = [jax.random.randint(jax.random.fold_in(stream_key, axis), (), 0, length) for axis, length in enumerate(values.shape)]
    main_axis = values.shape.index(max(values.shape))
    neighbour = spot[:main_axis] + [(spot[main_axis] + 1) % values.shape[main_axis]] + spot[main_axis + 1:]
    return values.at[tuple(spot)].set(least).at[tuple(neighbour)].set(top_value)


def block_levels(own_key, shape, cuts, smallest, top_value):
    level = 1.0
    for axis_at, parts in cuts:
        draws = jax.random.uniform(jax.random.fold_in(jax.random.fold_in(own_key, 6), axis_at), (parts,), jnp.float32, smallest / len(cuts), top_value / len(cuts))
        level = level * jnp.repeat(jnp.exp(draws), shape[axis_at] // parts).reshape((-1,) + (1,) * (len(shape) - 1 - axis_at))
    return level


def shared_out(rng, own, number, rows, number_of, top, limit, slope):
    order = jax.random.permutation(rng, number_of)
    crowded, common = portions_of(number_of, rows * top, limit, slope, True), portions_of(number_of, rows * top, limit, slope, False)
    places = jnp.arange(number_of)

    def named(sizes, offset_by):
        used = int((sizes > 0).sum())
        fixed = max(1, used // 4)
        moved = fixed + (places - fixed + offset_by * (used - fixed)) % max(1, number_of - fixed)
        return jnp.zeros((number_of,), jnp.int32).at[order[jnp.where(places < fixed, places, moved)]].set(jnp.asarray(sizes, jnp.int32))

    sizes = jnp.where(number % 4 == 0, named(crowded, number // 4), named(common, number - number // 4 - 1))
    mixed = jax.random.permutation(jax.random.fold_in(own, 3), number_of)
    donor, sink = mixed[0:number_of // 2 * 2:2], mixed[1:number_of // 2 * 2:2]
    margin = jnp.minimum(sizes[donor] - 1, limit - sizes[sink]) // 2
    margin = jnp.where((donor == order[0]) | (sink == order[0]) | (sizes[sink] == 0), 0, jnp.maximum(margin, 0))
    moved = jax.random.randint(jax.random.fold_in(own, 4), (number_of // 2,), 0, 1 << 20) % (margin + 1)
    sizes = sizes.at[donor].add(-moved).at[sink].add(moved)
    items = jnp.searchsorted(jnp.cumsum(sizes), jnp.arange(rows * top), side="right").astype(jnp.int32)
    listing = items.reshape(top, rows).T
    listing = listing[jax.random.permutation(jax.random.fold_in(own, 1), rows)]
    offset_by = jax.random.randint(jax.random.fold_in(own, 2), (rows, 1), 0, top)
    return jnp.take_along_axis(listing, (jnp.arange(top)[None, :] + offset_by) % top, axis=1)


def portions_of(amount, total, bound, lean, full):
    portions = [(1 << 20) // math.isqrt(rank ** lean) + 1 for rank in range(1, amount + 1)]
    largest = bound if full else min(bound, max(-(-total // amount), total * portions[0] // sum(portions)))
    least = 1 if total - largest >= amount - 1 else 0
    given, spare = [largest] + [least] * (amount - 1), total - largest - least * (amount - 1)
    while spare > 0:
        movable = [i for i in range(1, amount) if given[i] < largest] or [i for i in range(1, amount) if given[i] < bound]
        pool, left = sum([portions[i] for i in movable]), spare
        for i in movable:
            extra = min(bound - given[i], max(1, left * portions[i] // pool), spare)
            given[i] = given[i] + extra
            spare = spare - extra
    return np.array(given)


def scatter_about(rng, dims, spread, most, pieces=(), held_as=jnp.bfloat16):
    array = spread * jax.random.normal(rng, dims, jnp.float32)
    if pieces:
        array = array * block_levels(rng, dims, pieces, -0.22, 0.18)
    return jnp.clip(array, -most, most).astype(held_as)


def setup_inputs(seed: int = 0) -> dict:
    splits = jax.random.split(jax.random.key(seed), 7)
    front_entries = scatter_about(splits[0], (FRONTS, F, F), 1.0, 6.0, ((0, 8), (1, 16)))
    child_blocks = scatter_about(splits[1], (CHILDREN, BR, BC), 1.0, 6.0, ((0, 128),))
    dest_device_keys = jax.random.split(jax.random.fold_in(splits[2], 1), CHILDREN // K_DEV)
    dest_device_turns = jax.random.permutation(jax.random.fold_in(splits[2], 3), CHILDREN // K_DEV)
    dest_device = jax.vmap(lambda own, number: shared_out(jax.random.fold_in(splits[2], 2), own, number, K_DEV, DEVICES, 1, CAP, 2))(dest_device_keys, dest_device_turns).reshape((CHILDREN, 1))
    dest_tile = set_ends(jax.random.randint(splits[3], (CHILDREN,), 0, TILES_DEV), jax.random.fold_in(splits[3], 1), 0, TILES_DEV - 1).astype(jnp.int32)
    child_count = draw_child_count(jax.random.fold_in(splits[6], 71), 0)
    diag_inverse = draw_diag_inverse(jax.random.fold_in(splits[6], 71), 0)
    return {"front_entries": front_entries, "child_blocks": child_blocks, "dest_device": dest_device, "dest_tile": dest_tile, "child_count": child_count, "diag_inverse": diag_inverse}


def reference(front_entries, child_blocks, dest_device, dest_tile, child_count, diag_inverse):
    device_total = CHILDREN // K_DEV
    row_blocks = ROWS_DEV // BR
    col_blocks = F // BC
    active = (jnp.arange(CHILDREN, dtype=jnp.int32) % K_DEV) < jnp.repeat(child_count, K_DEV)
    target = dest_device[:, 0]
    owner_front = target // N_GRP
    tile_in_front = (target % N_GRP) * TILES_DEV + dest_tile
    outside = N_GRP * TILES_DEV
    source_blocks = child_blocks.reshape(device_total, K_DEV, BR, BC)

    def one_front(front_id):
        labels = jnp.where(active & (owner_front == front_id), tile_in_front, outside).astype(jnp.int32)
        labels = labels.reshape(device_total, K_DEV)

        def add_source(carry, inputs):
            blocks, marks = inputs
            return carry.at[marks].add(blocks.astype(jnp.float32), mode="drop"), None

        start = jnp.zeros((outside, BR, BC), jnp.float32)
        tiles, _ = lax.scan(add_source, start, (source_blocks, labels))
        added = tiles.reshape(N_GRP, row_blocks, col_blocks, BR, BC).transpose(0, 1, 3, 2, 4).reshape(F, F)
        assembled = front_entries[front_id].astype(jnp.float32) + added
        current = assembled.reshape(N_GRP, ROWS_DEV, N_GRP, ROWS_DEV)
        factors = []
        for step in range(PANELS):
            height = ROWS_DEV - step * PIV_DEV
            panel_cols = current[:, :, :, :PIV_DEV].reshape(N_GRP * height, PANEL)
            factor = jnp.dot(panel_cols, diag_inverse[front_id, step].T, precision=lax.Precision.HIGHEST, preferred_element_type=jnp.float32)
            shaped = factor.reshape(N_GRP, height, PANEL)
            padded = jnp.concatenate([jnp.zeros((N_GRP, step * PIV_DEV, PANEL), jnp.float32), shaped], axis=1)
            factors.append(padded.reshape(F, PANEL))
            rest = height - PIV_DEV
            lower = shaped[:, PIV_DEV:].reshape(N_GRP * rest, PANEL)
            trailing = current[:, PIV_DEV:, :, PIV_DEV:].reshape(N_GRP * rest, N_GRP * rest)
            update = jnp.dot(lower, lower.T, precision=lax.Precision.HIGHEST, preferred_element_type=jnp.float32)
            current = (trailing - update).reshape(N_GRP, rest, N_GRP, rest)
        final = current.reshape(TRAIL, TRAIL).astype(jnp.bfloat16)
        return final, jnp.stack(factors)

    schur, panel_factor = lax.map(one_front, jnp.arange(FRONTS, dtype=jnp.int32))
    return (schur, panel_factor)
```

```python
import functools

import jax
import jax.numpy as jnp
from jax import lax
from jax.experimental import pallas as pl
from jax.experimental.pallas import tpu as pltpu
from jax.sharding import PartitionSpec as P

LANE = 128
ROWTILE = 16
VMEM_LIMIT = 56 * 1024 * 1024
NT = (((1,), (1,)), ((), ()))


def params():
    return pltpu.CompilerParams(vmem_limit_bytes=VMEM_LIMIT)


def split(x):
    high = x.astype(jnp.bfloat16)
    return high, (x - high.astype(jnp.float32)).astype(jnp.bfloat16)


def dot_nt(a, b):
    return lax.dot_general(a, b, NT, preferred_element_type=jnp.float32)


def dot3(a, b):
    a_high, a_low = a
    b_high, b_low = b
    return dot_nt(a_high, b_high) + (dot_nt(a_high, b_low) + dot_nt(a_low, b_high))


def split_code(code):
    wide = code.astype(jnp.int32)
    high = ((wide + 128) >> 8) << 8
    low = wide - high
    return (
        high.astype(jnp.float32).astype(jnp.bfloat16),
        low.astype(jnp.float32).astype(jnp.bfloat16),
    )


def encode(x):
    rows = x.shape[0]
    largest = jnp.max(jnp.abs(x), axis=1, keepdims=True)
    exponent = jnp.ceil(jnp.log2(jnp.clip(largest, 1e-30, 1e38)))
    scaled = jnp.round(x * jnp.exp2(15.0 - exponent))
    code = jnp.clip(scaled, -32767.0, 32767.0).astype(jnp.int32).astype(jnp.int16)
    along = jnp.transpose(jnp.broadcast_to(exponent, (rows, LANE)))[:ROWTILE]
    return code, along.astype(jnp.int32).astype(jnp.int16)


def scale_of(exponent):
    return jnp.exp2(exponent.astype(jnp.int32).astype(jnp.float32) - 15.0)


def pack_first_kernel(count, position, blocks, labels, out, sem, label_sem):
    slots, rows, _ = blocks.shape

    def copy(i):
        at = position[i]
        return pltpu.make_async_copy(
            blocks.at[i, :, pl.ds(0, LANE)],
            out.at[at // 2, pl.ds(pl.multiple_of((at % 2) * rows, rows), rows), :],
            sem,
        )

    label_copy = pltpu.make_async_copy(labels, out.at[:, pl.ds(2 * rows, ROWTILE), :], label_sem)
    label_copy.start()

    @pl.loop(0, count[0])
    def _(i):
        copy(i).start()

    label_copy.wait()

    @pl.loop(0, count[0])
    def _(i):
        copy(i).wait()


def pack_rest_kernel(count, position, blocks, out, sem):
    width = blocks.shape[2]

    def copy(i):
        return pltpu.make_async_copy(
            blocks.at[i, :, pl.ds(LANE, width - LANE)], out.at[position[i]], sem
        )

    @pl.loop(0, count[0])
    def _(i):
        copy(i).start()

    @pl.loop(0, count[0])
    def _(i):
        copy(i).wait()


def gather_lanes(acc, start, width, groups):
    rows = acc.shape[1]
    per = LANE // width
    lane = lax.broadcasted_iota(jnp.int32, (rows, LANE), 1)
    out = []
    for tile in range(groups // per):
        total = None
        for k in range(per):
            piece = acc[tile * per + k]
            shift = (k * width - start) % LANE
            if shift:
                piece = pltpu.roll(piece, shift, 1)
            total = piece if total is None else jnp.where(lane >= k * width, piece, total)
        out.append(total)
    return jnp.concatenate(out, axis=1)


def panel_kernel(pivots, slot_count, label, arrived, front, inverse, factor, second, code, entries, acc, sem):
    groups, rows, _ = acc.shape
    block_rows = rows // groups
    width = front.shape[2] // groups

    def copy(c):
        return pltpu.make_async_copy(
            front.at[0, :, pl.ds(c * width, LANE)], entries.at[c], sem.at[c]
        )

    for c in range(groups):
        copy(c).start()
    for c in range(groups):
        copy(c).wait()
        acc[c] = entries[c].astype(jnp.float32)

    @pl.loop(0, slot_count)
    def _(s):
        at = label[s]

        @pl.when(at >= 0)
        def _():
            r, c = at // groups, at % groups
            where = pl.ds(pl.multiple_of(r * block_rows, block_rows), block_rows)
            source = pl.ds(pl.multiple_of((s % 2) * block_rows, block_rows), block_rows)
            acc[c, where, :] += arrived[s // 2, source, :].astype(jnp.float32)

    second[...] = gather_lanes(acc, pivots, pivots, groups)
    columns = gather_lanes(acc, 0, pivots, groups)
    result = dot3(split(columns), split(inverse[0, 0]))
    factor[...] = result
    codes, exponents = encode(result)
    code[: rows - pivots] = codes[pivots:]
    code[rows - pivots :] = exponents


def second_kernel(pivots, gathered, factor, second, inverse, factors, code, pivot_code, exponent, sem):
    groups = gathered.shape[0]
    rows, panel = factor.shape
    copies = [
        pltpu.make_async_copy(gathered.at[:, pl.ds(0, pivots), :], pivot_code, sem.at[0]),
        pltpu.make_async_copy(
            gathered.at[:, pl.ds(rows - pivots, ROWTILE), :], exponent, sem.at[1]
        ),
    ]
    for copy in copies:
        copy.start()
    factors[0, 0] = factor[...]
    for copy in copies:
        copy.wait()
    lane = lax.broadcasted_iota(jnp.int32, (ROWTILE, panel), 1)
    total = jnp.zeros((ROWTILE, panel), jnp.float32)
    for g in range(groups):
        scale = pltpu.roll(scale_of(exponent[g]), (g * pivots - pivots) % panel, 1)
        total = jnp.where((lane >= g * pivots) & (lane < (g + 1) * pivots), scale, total)
    pivot_rows = split_code(pivot_code[...].reshape(groups * pivots, panel))
    update = dot3(split(factor[pivots:]), pivot_rows) * total[:1]
    result = dot3(split(second[pivots:] - update), split(inverse[0, 0]))
    factors[0, 1, :pivots] = jnp.zeros((pivots, panel), jnp.float32)
    factors[0, 1, pivots:] = result
    codes, exponents = encode(jnp.concatenate([jnp.zeros((pivots, panel), jnp.float32), result], axis=0))
    code[: rows - 2 * pivots] = codes[2 * pivots :]
    code[rows - 2 * pivots :] = exponents


def update_kernel(pivots, factors, code0, code1, out, left, right):
    rows, panel = factors.shape[2], factors.shape[3]
    dead = 2 * pivots

    @pl.when(pl.program_id(0) == 0)
    def _():
        for k in range(2):
            high, low = split(factors[0, k, dead:])
            left[k, :, :panel] = high
            left[k, :, panel : 2 * panel] = high
            left[k, :, 2 * panel :] = low
            right[k] = jnp.zeros(right.shape[1:], jnp.bfloat16)

    total = None
    for k, code in enumerate((code0, code1)):
        first = (k + 1) * pivots
        kept = rows - first
        high, low = split_code(code[0, :kept])
        right[k, first:, :panel] = high
        right[k, first:, panel : 2 * panel] = low
        right[k, first:, 2 * panel :] = high
        scale = scale_of(code[0, kept : kept + ROWTILE])[:1]
        term = dot_nt(left[k], right[k]) * scale
        total = term if total is None else total + term
    out[...] = total


def finish_kernel(pivots, slot_count, label, first, rest, front, update, out, head, follow, buf):
    groups, block_rows, width = buf.shape
    dead = 2 * pivots
    step = pl.program_id(0)
    skipped = dead // block_rows

    @pl.when(step == 0)
    def _():
        @pl.loop(0, groups)
        def _(r):
            head[r] = -1

        @pl.loop(0, slot_count)
        def _(s):
            at = label[s]

            @pl.when(at >= 0)
            def _():
                r = at // groups
                follow[s] = head[r]
                head[r] = s

    for c in range(groups):
        columns = slice(c * width, (c + 1) * width)
        buf[c] = front[0, :, columns].astype(jnp.float32) - update[:, columns]

    def more(s):
        return s >= 0

    def add(s):
        c = label[s] % groups
        source = pl.ds(pl.multiple_of((s % 2) * block_rows, block_rows), block_rows)
        buf[c, :, :LANE] += first[s // 2, source, :].astype(jnp.float32)
        buf[c, :, LANE:] += rest[s].astype(jnp.float32)
        return follow[s]

    lax.while_loop(more, add, head[step + skipped])

    kept = width - dead
    for m in range(groups // 2):
        pair = jnp.concatenate([buf[2 * m][:, dead:], buf[2 * m + 1][:, dead:]], axis=1)
        out[0, :, 2 * m * kept : 2 * (m + 1) * kept] = pair.astype(jnp.bfloat16)


def local(front_entries, child_blocks, dest_device, dest_tile, child_count, diag_inverse):
    grp_total = lax.axis_size("grp")
    device_total = grp_total * lax.axis_size("front")
    axes = ("front", "grp")
    slots, block_rows, block_cols = child_blocks.shape
    _, rows, width = front_entries.shape
    panel = diag_inverse.shape[2]
    pivots = panel // grp_total
    slot_count = 2 * device_total
    rest_cols = block_cols - LANE
    hbm = pl.BlockSpec(memory_space=pl.ANY)
    smem = pl.BlockSpec(memory_space=pltpu.SMEM)
    vmem = pl.BlockSpec(memory_space=pltpu.VMEM)

    target = dest_device[:, 0]
    index = jnp.arange(slots, dtype=jnp.int32)
    same = (target[:, None] == target[None, :]) & (index[None, :] < index[:, None])
    occurrence = jnp.sum(same.astype(jnp.int32), axis=1)
    position = target * 2 + occurrence
    names = jnp.arange(slot_count, dtype=jnp.int32)
    live_label = jnp.where(index < child_count[0], dest_tile + 1, 0)
    labels = jnp.sum(
        jnp.where(position[None, :] == names[:, None], live_label[None, :], 0), axis=1
    ).reshape(device_total, 2)
    label_rows = jnp.concatenate(
        [
            jnp.broadcast_to(labels[:, :, None], (device_total, 2, LANE)),
            jnp.zeros((device_total, ROWTILE - 2, LANE), jnp.int32),
        ],
        axis=1,
    ).astype(jnp.bfloat16)

    first_out = pl.pallas_call(
        pack_first_kernel,
        out_shape=jax.ShapeDtypeStruct(
            (device_total, 2 * block_rows + ROWTILE, LANE), jnp.bfloat16
        ),
        in_specs=[smem, smem, hbm, hbm],
        out_specs=hbm,
        scratch_shapes=[pltpu.SemaphoreType.DMA, pltpu.SemaphoreType.DMA],
        compiler_params=params(),
        name="pack_first",
    )(child_count, position, child_blocks, label_rows)
    first = lax.all_to_all(first_out, axes, split_axis=0, concat_axis=0, tiled=True)
    rest_out = pl.pallas_call(
        pack_rest_kernel,
        out_shape=jax.ShapeDtypeStruct((slot_count, block_rows, rest_cols), jnp.bfloat16),
        in_specs=[smem, smem, hbm],
        out_specs=hbm,
        scratch_shapes=[pltpu.SemaphoreType.DMA],
        compiler_params=params(),
        name="pack_rest",
    )(child_count, position, child_blocks)
    first, rest_out = lax.optimization_barrier((first, rest_out))
    rest = lax.all_to_all(rest_out, axes, split_axis=0, concat_axis=0, tiled=True)
    label = first[:, 2 * block_rows : 2 * block_rows + 2, 0].astype(jnp.int32).reshape(-1) - 1

    code_rows = rows - pivots + ROWTILE
    inverse_spec = lambda k: pl.BlockSpec((1, 1, panel, panel), lambda i: (0, k, 0, 0))
    whole = lambda *shape: pl.BlockSpec(shape, lambda i: (0,) * len(shape))
    factor, second, code0 = pl.pallas_call(
        functools.partial(panel_kernel, pivots, slot_count),
        grid=(1,),
        out_shape=(
            jax.ShapeDtypeStruct((rows, panel), jnp.float32),
            jax.ShapeDtypeStruct((rows, panel), jnp.float32),
            jax.ShapeDtypeStruct((code_rows, panel), jnp.int16),
        ),
        in_specs=[smem, whole(*first.shape), hbm, inverse_spec(0)],
        out_specs=(whole(rows, panel), whole(rows, panel), whole(code_rows, panel)),
        scratch_shapes=[
            pltpu.VMEM((grp_total, rows, LANE), jnp.bfloat16),
            pltpu.VMEM((grp_total, rows, LANE), jnp.float32),
            pltpu.SemaphoreType.DMA((grp_total,)),
        ],
        compiler_params=params(),
        cost_estimate=pl.CostEstimate(flops=2 * 10**9, bytes_accessed=10 * 2**20, transcendentals=0),
        name="first_panel",
    )(label, first, front_entries, diag_inverse)
    gathered0 = lax.all_gather(code0, "grp", axis=0, tiled=False)

    code_rows1 = code_rows - pivots
    factors, code1 = pl.pallas_call(
        functools.partial(second_kernel, pivots),
        grid=(1,),
        out_shape=(
            jax.ShapeDtypeStruct((1, 2, rows, panel), jnp.float32),
            jax.ShapeDtypeStruct((code_rows1, panel), jnp.int16),
        ),
        in_specs=[hbm, whole(rows, panel), whole(rows, panel), inverse_spec(1)],
        out_specs=(whole(1, 2, rows, panel), whole(code_rows1, panel)),
        scratch_shapes=[
            pltpu.VMEM((grp_total, pivots, panel), jnp.int16),
            pltpu.VMEM((grp_total, ROWTILE, panel), jnp.int16),
            pltpu.SemaphoreType.DMA((2,)),
        ],
        compiler_params=params(),
        cost_estimate=pl.CostEstimate(flops=4 * 10**9, bytes_accessed=8 * 2**20, transcendentals=0),
        name="second_panel",
    )(gathered0, factor, second, diag_inverse)
    gathered1 = lax.all_gather(code1, "grp", axis=0, tiled=False)

    kept = rows - 2 * pivots
    update = pl.pallas_call(
        functools.partial(update_kernel, pivots),
        grid=(grp_total,),
        out_shape=jax.ShapeDtypeStruct((kept, width), jnp.float32),
        in_specs=[
            whole(1, 2, rows, panel),
            pl.BlockSpec((1, code_rows, panel), lambda i: (i, 0, 0)),
            pl.BlockSpec((1, code_rows1, panel), lambda i: (i, 0, 0)),
        ],
        out_specs=pl.BlockSpec((kept, rows), lambda i: (0, i)),
        scratch_shapes=[
            pltpu.VMEM((2, kept, 3 * panel), jnp.bfloat16),
            pltpu.VMEM((2, rows, 3 * panel), jnp.bfloat16),
        ],
        compiler_params=params(),
        cost_estimate=pl.CostEstimate(flops=20 * 10**9, bytes_accessed=32 * 2**20, transcendentals=0),
        name="update",
    )(factors, gathered0, gathered1)

    row_blocks = rows // block_rows
    skipped = 2 * pivots // block_rows
    schur = pl.pallas_call(
        functools.partial(finish_kernel, pivots, slot_count),
        grid=(row_blocks - skipped,),
        out_shape=jax.ShapeDtypeStruct((1, kept, grp_total * kept), jnp.bfloat16),
        in_specs=[
            smem,
            whole(*first.shape),
            whole(*rest.shape),
            pl.BlockSpec((1, block_rows, width), lambda i: (0, i + skipped, 0)),
            pl.BlockSpec((block_rows, width), lambda i: (i, 0)),
        ],
        out_specs=pl.BlockSpec((1, block_rows, grp_total * kept), lambda i: (0, i, 0)),
        scratch_shapes=[
            pltpu.SMEM((row_blocks,), jnp.int32),
            pltpu.SMEM((slot_count,), jnp.int32),
            pltpu.VMEM((width // block_cols, block_rows, block_cols), jnp.float32),
        ],
        compiler_params=params(),
        cost_estimate=pl.CostEstimate(flops=10**7, bytes_accessed=40 * 2**20, transcendentals=0),
        name="finish",
    )(label, first, rest, front_entries, update)
    return schur, factors


def solution(mesh):
    placed = (
        P("front", "grp", None),
        P(("front", "grp"), None, None),
        P(("front", "grp"), None),
        P(("front", "grp")),
        P(("front", "grp")),
        P("front", None, None, None),
    )
    return jax.shard_map(
        local,
        mesh=mesh,
        in_specs=placed,
        out_specs=(P("front", "grp", None), P("front", None, "grp", None)),
        check_vma=False,
    )
```

```python
import functools

import jax
import jax.numpy as jnp
from jax import lax
from jax.experimental import pallas as pl
from jax.experimental.pallas import tpu as pltpu
from jax.sharding import PartitionSpec as P

LANE = 128
ROWTILE = 16
VMEM_LIMIT = 56 * 1024 * 1024
NT = (((1,), (1,)), ((), ()))
NN = (((1,), (0,)), ((), ()))


def params():
    return pltpu.CompilerParams(vmem_limit_bytes=VMEM_LIMIT)


def split(x):
    high = x.astype(jnp.bfloat16)
    return high, (x - high.astype(jnp.float32)).astype(jnp.bfloat16)


def dot_nt(a, b, form=NT):
    return lax.dot_general(a, b, form, preferred_element_type=jnp.float32)


def dot3(a, b, form=NT):
    a_high, a_low = a
    b_high, b_low = b
    return dot_nt(a_high, b_high, form) + (
        dot_nt(a_high, b_low, form) + dot_nt(a_low, b_high, form)
    )


def split_code(code):
    wide = code.astype(jnp.int32)
    high = ((wide + 128) >> 8) << 8
    low = wide - high
    return (
        high.astype(jnp.float32).astype(jnp.bfloat16),
        low.astype(jnp.float32).astype(jnp.bfloat16),
    )


def encode(x):
    rows = x.shape[0]
    largest = jnp.max(jnp.abs(x), axis=1, keepdims=True)
    exponent = jnp.ceil(jnp.log2(jnp.clip(largest, 1e-30, 1e38)))
    scaled = jnp.round(x * jnp.exp2(15.0 - exponent))
    code = jnp.clip(scaled, -32767.0, 32767.0).astype(jnp.int32).astype(jnp.int16)
    along = jnp.transpose(jnp.broadcast_to(exponent, (rows, LANE)))[:ROWTILE]
    return code, along.astype(jnp.int32)


def scale_of(exponent):
    return jnp.exp2(exponent.astype(jnp.int32).astype(jnp.float32) - 15.0)


def pack_first_kernel(count, position, blocks, labels, out):
    rows = blocks.shape[1]
    out[:, 2 * rows :, :] = labels[...]

    @pl.loop(0, count[0])
    def _(i):
        at = position[i]
        out[at // 2, pl.ds(pl.multiple_of((at % 2) * rows, rows), rows), :] = blocks[i]


def pack_rest_kernel(count, position, blocks, out):
    @pl.loop(0, count[0])
    def _(i):
        out[position[i]] = blocks[i, :, LANE:]


def gather_lanes(acc, start, width, groups):
    rows = acc.shape[1]
    per = LANE // width
    lane = lax.broadcasted_iota(jnp.int32, (rows, LANE), 1)
    out = []
    for tile in range(groups // per):
        total = None
        for k in range(per):
            piece = acc[tile * per + k]
            shift = (k * width - start) % LANE
            if shift:
                piece = pltpu.roll(piece, shift, 1)
            total = piece if total is None else jnp.where(lane >= k * width, piece, total)
        out.append(total)
    return jnp.concatenate(out, axis=1)


def panel_kernel(
    pivots, slot_count, label, arrived, front, inverse, factor, second, middle, code, entries, acc, sem
):
    groups, rows, _ = acc.shape
    block_rows = rows // groups
    width = front.shape[2] // groups
    dead = 2 * pivots

    def copy(c):
        return pltpu.make_async_copy(
            front.at[0, :, pl.ds(c * width, LANE)], entries.at[c], sem.at[c]
        )

    for c in range(groups):
        copy(c).start()
    for c in range(groups):
        copy(c).wait()
        acc[c] = entries[c].astype(jnp.float32)

    @pl.loop(0, slot_count)
    def _(s):
        at = label[s]

        @pl.when(at >= 0)
        def _():
            r, c = at // groups, at % groups
            where = pl.ds(pl.multiple_of(r * block_rows, block_rows), block_rows)
            source = pl.ds(pl.multiple_of((s % 2) * block_rows, block_rows), block_rows)
            acc[c, where, :] += arrived[s // 2, source, :].astype(jnp.float32)

    middle[...] = acc[:, dead:, :]
    later = gather_lanes(acc, pivots, pivots, groups)
    second[...] = later
    columns = gather_lanes(acc, 0, pivots, groups)
    result = dot3(split(columns), split(inverse[0, 0]))
    factor[...] = result
    codes, exponents = encode(result)
    later_codes, later_exponents = encode(later)
    kept, kept_later = rows - pivots, rows - dead
    code[:kept] = codes[pivots:]
    code[kept : kept + kept_later] = later_codes[dead:]
    row = lax.broadcasted_iota(jnp.int32, exponents.shape, 0)
    code[kept + kept_later :] = jnp.where(row == 0, exponents, later_exponents).astype(jnp.int16)


def left_kernel(pivots, gathered, factor, second, inverse, factors, left, pivot_code, exponent, sem):
    groups, code_rows, _ = gathered.shape
    rows, panel = factor.shape
    copies = [
        pltpu.make_async_copy(gathered.at[:, pl.ds(0, pivots), :], pivot_code, sem.at[0]),
        pltpu.make_async_copy(
            gathered.at[:, pl.ds(code_rows - ROWTILE, ROWTILE), :], exponent, sem.at[1]
        ),
    ]
    for copy in copies:
        copy.start()
    factors[0, 0] = factor[...]
    for copy in copies:
        copy.wait()
    lane = lax.broadcasted_iota(jnp.int32, (ROWTILE, panel), 1)
    total = jnp.zeros((ROWTILE, panel), jnp.float32)
    for g in range(groups):
        scale = pltpu.roll(scale_of(exponent[g]), (g * pivots - pivots) % panel, 1)
        total = jnp.where((lane >= g * pivots) & (lane < (g + 1) * pivots), scale, total)
    scale = total[:1]
    pivot_rows = split_code(pivot_code[...].reshape(groups * pivots, panel))
    inverse_parts = split(inverse[0, 0])
    first = factor[pivots:]
    update = dot3(split(first), pivot_rows) * scale
    result = dot3(split(second[pivots:] - update), inverse_parts)
    factors[0, 1, :pivots] = jnp.zeros((pivots, panel), jnp.float32)
    factors[0, 1, pivots:] = result
    own = dot3(split(result[pivots:]), inverse_parts, NN)
    mixed = first[pivots:] - dot3(split(own * scale), pivot_rows, NN)
    for k, part in enumerate((mixed, own)):
        high, low = split(part)
        left[k, :, :panel] = high
        left[k, :, panel : 2 * panel] = high
        left[k, :, 2 * panel :] = low


def update_kernel(pivots, slot_count, label, left, code, front, middle, out, head, follow, right):
    rows, panel = right.shape[1], code.shape[2]
    groups = head.shape[0]
    dead = 2 * pivots

    @pl.when(pl.program_id(0) == 0)
    def _():
        right[...] = jnp.zeros(right.shape, jnp.bfloat16)

        @pl.loop(0, groups)
        def _(r):
            head[r] = -1

        @pl.loop(0, slot_count)
        def _(s):
            at = label[s]

            @pl.when(at >= 0)
            def _():
                r = at // groups
                follow[s] = head[r]
                head[r] = s

    kept = (rows - pivots, rows - dead)
    starts = (0, kept[0])
    sides = []
    for d in range(2):
        scale = scale_of(code[d, kept[0] + kept[1] :])
        columns = slice(d * rows + LANE, (d + 1) * rows)
        total = jnp.concatenate(
            [middle[d], front[0, dead:, columns].astype(jnp.float32)], axis=1
        )
        for k in range(2):
            high, low = split_code(code[d, starts[k] : starts[k] + kept[k]])
            right[k, rows - kept[k] :, :panel] = high
            right[k, rows - kept[k] :, panel : 2 * panel] = low
            right[k, rows - kept[k] :, 2 * panel :] = high
            total = total - dot_nt(left[k], right[k]) * scale[k : k + 1]
        sides.append(total[:, dead:])
    out[...] = jnp.concatenate(sides, axis=1)


def finish_kernel(label, head, follow, rest, trailing, out, buf):
    groups = head.shape[0]
    _, block_rows, width = rest.shape
    pairs, _, pair_width = buf.shape
    kept = pair_width // 2
    step = pl.program_id(0)
    skipped = groups - pl.num_programs(0)
    for m in range(pairs):
        buf[m] = trailing[:, m * pair_width : (m + 1) * pair_width]

    def more(s):
        return s >= 0

    def add(s):
        c = label[s] % groups
        m = c // 2
        block = rest[s].astype(jnp.float32)
        offset = kept - width

        @pl.when(c % 2 == 0)
        def _():
            pad = jnp.zeros((block_rows, offset), jnp.float32)
            buf[m, :, : width + 2 * offset] += jnp.concatenate([pad, block, pad], axis=1)

        @pl.when(c % 2 == 1)
        def _():
            buf[m, :, kept + offset :] += block

        return follow[s]

    lax.while_loop(more, add, head[step + skipped])
    for m in range(pairs):
        out[0, :, m * pair_width : (m + 1) * pair_width] = buf[m].astype(jnp.bfloat16)


def local(front_entries, child_blocks, dest_device, dest_tile, child_count, diag_inverse):
    grp_total = lax.axis_size("grp")
    device_total = grp_total * lax.axis_size("front")
    axes = ("front", "grp")
    slots, block_rows, block_cols = child_blocks.shape
    _, rows, width = front_entries.shape
    panel = diag_inverse.shape[2]
    pivots = panel // grp_total
    slot_count = 2 * device_total
    rest_cols = block_cols - LANE
    hbm = pl.BlockSpec(memory_space=pl.ANY)
    smem = pl.BlockSpec(memory_space=pltpu.SMEM)
    whole = lambda *shape: pl.BlockSpec(shape, lambda i: (0,) * len(shape))

    target = dest_device[:, 0]
    index = jnp.arange(slots, dtype=jnp.int32)
    same = (target[:, None] == target[None, :]) & (index[None, :] < index[:, None])
    occurrence = jnp.sum(same.astype(jnp.int32), axis=1)
    position = target * 2 + occurrence
    names = jnp.arange(slot_count, dtype=jnp.int32)
    live_label = jnp.where(index < child_count[0], dest_tile + 1, 0)
    labels = jnp.sum(
        jnp.where(position[None, :] == names[:, None], live_label[None, :], 0), axis=1
    ).reshape(device_total, 2)
    label_rows = jnp.concatenate(
        [
            jnp.broadcast_to(labels[:, :, None], (device_total, 2, LANE)),
            jnp.zeros((device_total, ROWTILE - 2, LANE), jnp.int32),
        ],
        axis=1,
    ).astype(jnp.bfloat16)

    first_out = pl.pallas_call(
        pack_first_kernel,
        grid=(1,),
        out_shape=jax.ShapeDtypeStruct(
            (device_total, 2 * block_rows + ROWTILE, LANE), jnp.bfloat16
        ),
        in_specs=[smem, smem, whole(slots, block_rows, LANE), whole(*label_rows.shape)],
        out_specs=whole(device_total, 2 * block_rows + ROWTILE, LANE),
        compiler_params=params(),
        name="pack_first",
    )(child_count, position, child_blocks, label_rows)
    first = lax.all_to_all(first_out, axes, split_axis=0, concat_axis=0, tiled=True)
    rest_out = pl.pallas_call(
        pack_rest_kernel,
        grid=(1,),
        out_shape=jax.ShapeDtypeStruct((slot_count, block_rows, rest_cols), jnp.bfloat16),
        in_specs=[smem, smem, whole(*child_blocks.shape)],
        out_specs=whole(slot_count, block_rows, rest_cols),
        compiler_params=params(),
        cost_estimate=pl.CostEstimate(flops=0, bytes_accessed=10 * 2**20, transcendentals=0),
        name="pack_rest",
    )(child_count, position, child_blocks)
    first, rest_out = lax.optimization_barrier((first, rest_out))
    label = first[:, 2 * block_rows : 2 * block_rows + 2, 0].astype(jnp.int32).reshape(-1) - 1

    kept = rows - 2 * pivots
    code_rows = (rows - pivots) + kept + ROWTILE
    inverse_spec = lambda k: pl.BlockSpec((1, 1, panel, panel), lambda i: (0, k, 0, 0))
    factor, second, middle, code = pl.pallas_call(
        functools.partial(panel_kernel, pivots, slot_count),
        grid=(1,),
        out_shape=(
            jax.ShapeDtypeStruct((rows, panel), jnp.float32),
            jax.ShapeDtypeStruct((rows, panel), jnp.float32),
            jax.ShapeDtypeStruct((grp_total, kept, LANE), jnp.float32),
            jax.ShapeDtypeStruct((code_rows, panel), jnp.int16),
        ),
        in_specs=[smem, whole(*first.shape), hbm, inverse_spec(0)],
        out_specs=(
            whole(rows, panel),
            whole(rows, panel),
            whole(grp_total, kept, LANE),
            whole(code_rows, panel),
        ),
        scratch_shapes=[
            pltpu.VMEM((grp_total, rows, LANE), jnp.bfloat16),
            pltpu.VMEM((grp_total, rows, LANE), jnp.float32),
            pltpu.SemaphoreType.DMA((grp_total,)),
        ],
        compiler_params=params(),
        cost_estimate=pl.CostEstimate(flops=2 * 10**9, bytes_accessed=10 * 2**20, transcendentals=0),
        name="panels",
    )(label, first, front_entries, diag_inverse)
    gathered = lax.all_gather(code, "grp", axis=0, tiled=False)

    gathered, rest_out = lax.optimization_barrier((gathered, rest_out))
    rest = lax.all_to_all(rest_out, axes, split_axis=0, concat_axis=0, tiled=True)

    factors, left = pl.pallas_call(
        functools.partial(left_kernel, pivots),
        grid=(1,),
        out_shape=(
            jax.ShapeDtypeStruct((1, 2, rows, panel), jnp.float32),
            jax.ShapeDtypeStruct((2, kept, 3 * panel), jnp.bfloat16),
        ),
        in_specs=[hbm, whole(rows, panel), whole(rows, panel), inverse_spec(1)],
        out_specs=(whole(1, 2, rows, panel), whole(2, kept, 3 * panel)),
        scratch_shapes=[
            pltpu.VMEM((grp_total, pivots, panel), jnp.int16),
            pltpu.VMEM((grp_total, ROWTILE, panel), jnp.int16),
            pltpu.SemaphoreType.DMA((2,)),
        ],
        compiler_params=params(),
        cost_estimate=pl.CostEstimate(flops=4 * 10**9, bytes_accessed=8 * 2**20, transcendentals=0),
        name="left_factors",
    )(gathered, factor, second, diag_inverse)

    trailing, head, follow = pl.pallas_call(
        functools.partial(update_kernel, pivots, slot_count),
        grid=(grp_total // 2,),
        out_shape=(
            jax.ShapeDtypeStruct((kept, grp_total * kept), jnp.float32),
            jax.ShapeDtypeStruct((rows // block_rows,), jnp.int32),
            jax.ShapeDtypeStruct((slot_count,), jnp.int32),
        ),
        in_specs=[
            smem,
            whole(2, kept, 3 * panel),
            pl.BlockSpec((2, code_rows, panel), lambda i: (i, 0, 0)),
            pl.BlockSpec((1, rows, 2 * rows), lambda i: (0, 0, i)),
            pl.BlockSpec((2, kept, LANE), lambda i: (i, 0, 0)),
        ],
        out_specs=(pl.BlockSpec((kept, 2 * kept), lambda i: (0, i)), smem, smem),
        scratch_shapes=[pltpu.VMEM((2, rows, 3 * panel), jnp.bfloat16)],
        compiler_params=params(),
        cost_estimate=pl.CostEstimate(flops=20 * 10**9, bytes_accessed=40 * 2**20, transcendentals=0),
        name="update",
    )(label, left, gathered, front_entries, middle)

    row_blocks = rows // block_rows
    skipped = 2 * pivots // block_rows
    schur = pl.pallas_call(
        finish_kernel,
        grid=(row_blocks - skipped,),
        out_shape=jax.ShapeDtypeStruct((1, kept, grp_total * kept), jnp.bfloat16),
        in_specs=[
            smem,
            smem,
            smem,
            whole(*rest.shape),
            pl.BlockSpec((block_rows, grp_total * kept), lambda i: (i, 0)),
        ],
        out_specs=pl.BlockSpec((1, block_rows, grp_total * kept), lambda i: (0, i, 0)),
        scratch_shapes=[pltpu.VMEM((grp_total // 2, block_rows, 2 * kept), jnp.float32)],
        compiler_params=params(),
        cost_estimate=pl.CostEstimate(flops=10**7, bytes_accessed=30 * 2**20, transcendentals=0),
        name="finish",
    )(label, head, follow, rest, trailing)
    return schur, factors


def solution(mesh):
    placed = (
        P("front", "grp", None),
        P(("front", "grp"), None, None),
        P(("front", "grp"), None),
        P(("front", "grp")),
        P(("front", "grp")),
        P("front", None, None, None),
    )
    return jax.shard_map(
        local,
        mesh=mesh,
        in_specs=placed,
        out_specs=(P("front", "grp", None), P("front", None, "grp", None)),
        check_vma=False,
    )
```

```python
import functools

import jax
import jax.numpy as jnp
from jax import lax
from jax.experimental import pallas as pl
from jax.experimental.pallas import tpu as pltpu
from jax.sharding import PartitionSpec as P

LANE = 128
ROWTILE = 16
LABELROWS = 8
VMEM_LIMIT = 56 * 1024 * 1024
NT = (((1,), (1,)), ((), ()))
NN = (((1,), (0,)), ((), ()))


def params():
    return pltpu.CompilerParams(vmem_limit_bytes=VMEM_LIMIT)


def split(x):
    high = x.astype(jnp.bfloat16)
    return high, (x - high.astype(jnp.float32)).astype(jnp.bfloat16)


def dot_nt(a, b, form=NT):
    return lax.dot_general(a, b, form, preferred_element_type=jnp.float32)


def dot3(a, b, form=NT):
    a_high, a_low = a
    b_high, b_low = b
    return dot_nt(a_high, b_high, form) + (
        dot_nt(a_high, b_low, form) + dot_nt(a_low, b_high, form)
    )


def split_code(code):
    wide = code.astype(jnp.int32)
    high = ((wide + 128) >> 8) << 8
    low = wide - high
    return (
        high.astype(jnp.float32).astype(jnp.bfloat16),
        low.astype(jnp.float32).astype(jnp.bfloat16),
    )


def encode(x):
    rows = x.shape[0]
    largest = jnp.max(jnp.abs(x), axis=1, keepdims=True)
    exponent = jnp.ceil(jnp.log2(jnp.clip(largest, 1e-30, 1e38)))
    scaled = jnp.round(x * jnp.exp2(15.0 - exponent))
    code = jnp.clip(scaled, -32767.0, 32767.0).astype(jnp.int32).astype(jnp.int16)
    along = jnp.transpose(jnp.broadcast_to(exponent, (rows, LANE)))[:ROWTILE]
    return code, along.astype(jnp.int32)


def scale_of(exponent):
    return jnp.exp2(exponent.astype(jnp.int32).astype(jnp.float32) - 15.0)


def pack_first_kernel(count, target, tile, blocks, out, position, load, marks, sem):
    devices = out.shape[0]
    slots, rows, _ = blocks.shape
    copy = pltpu.make_async_copy(blocks.at[:, :, pl.ds(0, LANE)], load, sem)
    copy.start()

    @pl.loop(0, devices, unroll=8)
    def _(t):
        marks[2, t] = 2 * t
        marks[0, t] = 0
        marks[1, t] = 0

    @pl.loop(0, slots, unroll=4)
    def _(i):
        t = target[i]
        at = marks[2, t]
        marks[2, t] = at + 1
        position[i] = at
        marks[at % 2, t] = jnp.where(i < count[0], tile[i] + 1, 0)

    row = lax.broadcasted_iota(jnp.int32, (LABELROWS, LANE), 0)

    @pl.loop(0, devices, unroll=8)
    def _(t):
        both = jnp.where(row == 0, marks[0, t], jnp.where(row == 1, marks[1, t], 0))
        out[t, 2 * rows :, :] = both.astype(jnp.float32).astype(jnp.bfloat16)

    copy.wait()

    @pl.loop(0, slots, unroll=4)
    def _(i):
        at = position[i]
        out[at // 2, pl.ds(pl.multiple_of((at % 2) * rows, rows), rows), :] = load[i]


def pack_rest_kernel(position, blocks, front, middle, rest, entries, sem):
    groups = entries.shape[0]
    width = front.shape[2] // groups

    def copy(c):
        return pltpu.make_async_copy(
            front.at[0, :, pl.ds(c * width, LANE)], entries.at[c], sem.at[c]
        )

    for c in range(groups):
        copy(c).start()

    @pl.loop(0, blocks.shape[0], unroll=2)
    def _(i):
        at = position[i]
        middle[at] = blocks[i, :, LANE : 2 * LANE]
        rest[at] = blocks[i, :, 2 * LANE :]

    for c in range(groups):
        copy(c).wait()


def gather_lanes(acc, rows, start, width, groups):
    per = LANE // width
    lane = lax.broadcasted_iota(jnp.int32, (rows, LANE), 1)
    out = []
    for tile in range(groups // per):
        total = None
        for k in range(per):
            piece = acc[tile * per + k, :rows]
            shift = (k * width - start) % LANE
            if shift:
                piece = pltpu.roll(piece, shift, 1)
            total = piece if total is None else jnp.where(lane >= k * width, piece, total)
        out.append(total)
    return jnp.concatenate(out, axis=1)


def panel_kernel(
    pivots, arrived, entries, inverse, factor, second, code, label, acc, marks, load, later, result, sem
):
    groups, rows, _ = entries.shape
    sources = arrived.shape[0]
    block_rows = rows // groups
    dead = 2 * pivots
    inverse_copy = pltpu.make_async_copy(inverse.at[0, 0], load, sem.at[1])
    inverse_copy.start()

    shape = (sources, LABELROWS, LANE)
    own = lax.broadcasted_iota(jnp.int32, shape, 0) == lax.broadcasted_iota(jnp.int32, shape, 2)
    sent = arrived[:, 2 * block_rows :, :].astype(jnp.float32)
    label[...] = jnp.sum(jnp.where(own, sent, 0.0), axis=0).astype(jnp.int32) - 1
    copy = pltpu.make_async_copy(label, marks, sem.at[0])
    copy.start()
    acc[:, :rows] = entries[...].astype(jnp.float32)
    copy.wait()

    @pl.loop(0, sources, unroll=4)
    def _(source):
        for k in range(2):
            at = marks[k, source]
            at = jnp.where(at < 0, groups * groups, at)
            r, c = at // groups, at % groups
            where = pl.ds(pl.multiple_of(r * block_rows, block_rows), block_rows)
            block = arrived[source, k * block_rows : (k + 1) * block_rows, :]
            acc[c, where, :] += block.astype(jnp.float32)

    later[...] = gather_lanes(acc, rows, pivots, pivots, groups)
    later_copy = pltpu.make_async_copy(later, second, sem.at[2])
    later_copy.start()
    columns = gather_lanes(acc, rows, 0, pivots, groups)
    inverse_copy.wait()
    result[...] = dot3(split(columns), split(load[...]))
    result_copy = pltpu.make_async_copy(result, factor, sem.at[3])
    result_copy.start()
    codes, exponents = encode(result[...])
    later_codes, later_exponents = encode(later[...])
    kept, kept_later = rows - pivots, rows - dead
    code[:kept] = codes[pivots:]
    code[kept : kept + kept_later] = later_codes[dead:]
    row = lax.broadcasted_iota(jnp.int32, exponents.shape, 0)
    code[kept + kept_later :] = jnp.where(row == 0, exponents, later_exponents).astype(jnp.int16)
    later_copy.wait()
    result_copy.wait()


def left_kernel(pivots, gathered, factor, second, inverse, factors, left, pivot_code, exponent, sem):
    groups, code_rows, _ = gathered.shape
    rows, panel = factor.shape
    copies = [
        pltpu.make_async_copy(gathered.at[:, pl.ds(0, pivots), :], pivot_code, sem.at[0]),
        pltpu.make_async_copy(
            gathered.at[:, pl.ds(code_rows - ROWTILE, ROWTILE), :], exponent, sem.at[1]
        ),
    ]
    for copy in copies:
        copy.start()
    factors[0, 0] = factor[...]
    for copy in copies:
        copy.wait()
    lane = lax.broadcasted_iota(jnp.int32, (ROWTILE, panel), 1)
    total = jnp.zeros((ROWTILE, panel), jnp.float32)
    for g in range(groups):
        scale = pltpu.roll(scale_of(exponent[g]), (g * pivots - pivots) % panel, 1)
        total = jnp.where((lane >= g * pivots) & (lane < (g + 1) * pivots), scale, total)
    scale = total[:1]
    pivot_rows = split_code(pivot_code[...].reshape(groups * pivots, panel))
    inverse_parts = split(inverse[0, 0])
    first = factor[pivots:]
    update = dot3(split(first), pivot_rows) * scale
    result = dot3(split(second[pivots:] - update), inverse_parts)
    factors[0, 1, :pivots] = jnp.zeros((pivots, panel), jnp.float32)
    factors[0, 1, pivots:] = result
    own = dot3(split(result[pivots:]), inverse_parts, NN)
    mixed = first[pivots:] - dot3(split(own * scale), pivot_rows, NN)
    for k, part in enumerate((mixed, own)):
        high, low = split(part)
        left[k, :, :panel] = high
        left[k, :, panel : 2 * panel] = high
        left[k, :, 2 * panel :] = low


def list_blocks(label, groups, start, order, column, head, follow):
    sources = label.shape[1]

    @pl.loop(0, groups)
    def _(r):
        start[r] = 0
        head[r] = -1

    def each(act):
        @pl.loop(0, sources)
        def _(source):
            for k in range(2):
                at = label[k, source]

                @pl.when(at >= 0)
                def _():
                    act(2 * source + k, at // groups, at % groups)

    def count(slot, r, c):
        start[r] += 1
        follow[slot] = head[c]
        head[c] = slot

    def place(slot, r, c):
        at = start[r] - 1
        start[r] = at
        order[at] = slot
        column[at] = c

    each(count)
    start[groups] = 0

    @pl.loop(0, groups)
    def _(r):
        start[groups] += start[r]
        start[r] = start[groups]

    each(place)


def update_kernel(
    pivots, label, left, code, front, first, middle, done, open_, start, order, column, head, follow, right, acc
):
    rows, panel = right.shape[1], code.shape[2]
    groups = head.shape[0]
    block_rows = rows // groups
    dead = 2 * pivots
    step = pl.program_id(0)

    @pl.when(step == 0)
    def _():
        right[...] = jnp.zeros(right.shape, jnp.bfloat16)
        list_blocks(label, groups, start, order, column, head, follow)

    for d in range(2):
        acc[d] = front[0, :, d * rows : d * rows + 2 * LANE].astype(jnp.float32)

        def add(slot, d=d):
            k = slot % 2
            r = label[k, slot // 2] // groups
            where = pl.ds(pl.multiple_of(r * block_rows, block_rows), block_rows)
            source = pl.ds(pl.multiple_of(k * block_rows, block_rows), block_rows)
            acc[d, where, :LANE] += first[slot // 2, source, :].astype(jnp.float32)
            acc[d, where, LANE:] += middle[slot].astype(jnp.float32)
            return follow[slot]

        lax.while_loop(lambda slot: slot >= 0, add, head[2 * step + d])

    kept = (rows - pivots, rows - dead)
    starts = (0, kept[0])
    for d in range(2):
        scale = scale_of(code[d, kept[0] + kept[1] :])
        columns = slice(d * rows + 2 * LANE, (d + 1) * rows)
        total = jnp.concatenate(
            [acc[d, dead:], front[0, dead:, columns].astype(jnp.float32)], axis=1
        )
        for k in range(2):
            high, low = split_code(code[d, starts[k] : starts[k] + kept[k]])
            right[k, rows - kept[k] :, :panel] = high
            right[k, rows - kept[k] :, panel : 2 * panel] = low
            right[k, rows - kept[k] :, 2 * panel :] = high
            total = total - dot_nt(left[k], right[k]) * scale[k : k + 1]
        done[d] = total[:, : 2 * LANE].astype(jnp.bfloat16)
        open_[d] = total[:, 2 * LANE :]


def finish_kernel(pivots, start, order, column, rest, done, open_, out, acc):
    groups, step_rows, _ = acc.shape
    block_rows = rest.shape[1]
    dead = 2 * pivots
    kept = 4 * LANE - dead
    per = step_rows // block_rows
    row = pl.program_id(0) * per + groups - pl.num_programs(0) * per
    acc[...] = jnp.zeros(acc.shape, jnp.float32)
    for p in range(per):

        @pl.loop(start[row + p], start[row + p + 1])
        def _(i):
            block = rest[order[i]].astype(jnp.float32)
            acc[column[i], p * block_rows : (p + 1) * block_rows, :] += block

    for m in range(groups // 2):
        sides = []
        for c in (2 * m, 2 * m + 1):
            sides.append(done[c, :, dead:])
            sides.append((open_[c] + acc[c]).astype(jnp.bfloat16))
        pair = jnp.concatenate(sides, axis=1)
        out[0, :, 2 * m * kept : 2 * (m + 1) * kept] = pair


def local(front_entries, child_blocks, dest_device, dest_tile, child_count, diag_inverse):
    grp_total = lax.axis_size("grp")
    device_total = grp_total * lax.axis_size("front")
    axes = ("front", "grp")
    slots, block_rows, block_cols = child_blocks.shape
    _, rows, width = front_entries.shape
    panel = diag_inverse.shape[2]
    pivots = panel // grp_total
    slot_count = 2 * device_total
    rest_cols = block_cols - 2 * LANE
    hbm = pl.BlockSpec(memory_space=pl.ANY)
    smem = pl.BlockSpec(memory_space=pltpu.SMEM)
    whole = lambda *shape: pl.BlockSpec(shape, lambda i: (0,) * len(shape))

    first_rows = 2 * block_rows + LABELROWS
    first_out, position = pl.pallas_call(
        pack_first_kernel,
        grid=(1,),
        out_shape=(
            jax.ShapeDtypeStruct((device_total, first_rows, LANE), jnp.bfloat16),
            jax.ShapeDtypeStruct((slots,), jnp.int32),
        ),
        in_specs=[smem, smem, smem, hbm],
        out_specs=(whole(device_total, first_rows, LANE), smem),
        scratch_shapes=[
            pltpu.VMEM((slots, block_rows, LANE), jnp.bfloat16),
            pltpu.SMEM((3, device_total), jnp.int32),
            pltpu.SemaphoreType.DMA,
        ],
        compiler_params=params(),
        name="pack_first",
    )(child_count, dest_device.reshape(slots), dest_tile, child_blocks)
    first = lax.all_to_all(first_out, axes, split_axis=0, concat_axis=0, tiled=True)
    middle_out, rest_out, entries = pl.pallas_call(
        pack_rest_kernel,
        grid=(1,),
        out_shape=(
            jax.ShapeDtypeStruct((slot_count, block_rows, LANE), jnp.bfloat16),
            jax.ShapeDtypeStruct((slot_count, block_rows, rest_cols), jnp.bfloat16),
            jax.ShapeDtypeStruct((grp_total, rows, LANE), jnp.bfloat16),
        ),
        in_specs=[smem, whole(*child_blocks.shape), hbm],
        out_specs=(
            whole(slot_count, block_rows, LANE),
            whole(slot_count, block_rows, rest_cols),
            whole(grp_total, rows, LANE),
        ),
        scratch_shapes=[pltpu.SemaphoreType.DMA((grp_total,))],
        compiler_params=params(),
        cost_estimate=pl.CostEstimate(flops=0, bytes_accessed=16 * 2**20, transcendentals=0),
        name="pack_rest",
    )(position, child_blocks, front_entries)
    middle = lax.all_to_all(middle_out, axes, split_axis=0, concat_axis=0, tiled=True)
    first, rest_out, entries = lax.optimization_barrier((first, rest_out, entries))

    kept = rows - 2 * pivots
    code_rows = (rows - pivots) + kept + ROWTILE
    inverse_spec = lambda k: pl.BlockSpec((1, 1, panel, panel), lambda i: (0, k, 0, 0))
    factor, second, code, label = pl.pallas_call(
        functools.partial(panel_kernel, pivots),
        grid=(1,),
        out_shape=(
            jax.ShapeDtypeStruct((rows, panel), jnp.float32),
            jax.ShapeDtypeStruct((rows, panel), jnp.float32),
            jax.ShapeDtypeStruct((code_rows, panel), jnp.int16),
            jax.ShapeDtypeStruct((LABELROWS, LANE), jnp.int32),
        ),
        in_specs=[whole(*first.shape), whole(*entries.shape), hbm],
        out_specs=(hbm, hbm, whole(code_rows, panel), whole(LABELROWS, LANE)),
        scratch_shapes=[
            pltpu.VMEM((grp_total, rows + block_rows, LANE), jnp.float32),
            pltpu.SMEM((LABELROWS, LANE), jnp.int32),
            pltpu.VMEM((panel, panel), jnp.float32),
            pltpu.VMEM((rows, panel), jnp.float32),
            pltpu.VMEM((rows, panel), jnp.float32),
            pltpu.SemaphoreType.DMA((4,)),
        ],
        compiler_params=params(),
        cost_estimate=pl.CostEstimate(flops=2 * 10**9, bytes_accessed=10 * 2**20, transcendentals=0),
        name="panels",
    )(first, entries, diag_inverse)
    gathered = lax.all_gather(code, "grp", axis=0, tiled=False)

    gathered, rest_out = lax.optimization_barrier((gathered, rest_out))
    rest = lax.all_to_all(rest_out, axes, split_axis=0, concat_axis=0, tiled=True)

    factors, left = pl.pallas_call(
        functools.partial(left_kernel, pivots),
        grid=(1,),
        out_shape=(
            jax.ShapeDtypeStruct((1, 2, rows, panel), jnp.float32),
            jax.ShapeDtypeStruct((2, kept, 3 * panel), jnp.bfloat16),
        ),
        in_specs=[hbm, whole(rows, panel), whole(rows, panel), inverse_spec(1)],
        out_specs=(whole(1, 2, rows, panel), whole(2, kept, 3 * panel)),
        scratch_shapes=[
            pltpu.VMEM((grp_total, pivots, panel), jnp.int16),
            pltpu.VMEM((grp_total, ROWTILE, panel), jnp.int16),
            pltpu.SemaphoreType.DMA((2,)),
        ],
        compiler_params=params(),
        cost_estimate=pl.CostEstimate(flops=4 * 10**9, bytes_accessed=8 * 2**20, transcendentals=0),
        name="left_factors",
    )(gathered, factor, second, diag_inverse)

    row_blocks = rows // block_rows
    lists = (row_blocks + 1, slot_count, slot_count)
    done, open_, *lists = pl.pallas_call(
        functools.partial(update_kernel, pivots),
        grid=(grp_total // 2,),
        out_shape=(
            jax.ShapeDtypeStruct((grp_total, kept, 2 * LANE), jnp.bfloat16),
            jax.ShapeDtypeStruct((grp_total, kept, rest_cols), jnp.float32),
            *(jax.ShapeDtypeStruct((length,), jnp.int32) for length in lists),
        ),
        in_specs=[
            smem,
            whole(2, kept, 3 * panel),
            pl.BlockSpec((2, code_rows, panel), lambda i: (i, 0, 0)),
            pl.BlockSpec((1, rows, 2 * rows), lambda i: (0, 0, i)),
            whole(*first.shape),
            whole(*middle.shape),
        ],
        out_specs=(
            pl.BlockSpec((2, kept, 2 * LANE), lambda i: (i, 0, 0)),
            pl.BlockSpec((2, kept, rest_cols), lambda i: (i, 0, 0)),
            smem,
            smem,
            smem,
        ),
        scratch_shapes=[
            pltpu.SMEM((row_blocks,), jnp.int32),
            pltpu.SMEM((slot_count,), jnp.int32),
            pltpu.VMEM((2, rows, 3 * panel), jnp.bfloat16),
            pltpu.VMEM((2, rows, 2 * LANE), jnp.float32),
        ],
        compiler_params=params(),
        cost_estimate=pl.CostEstimate(flops=20 * 10**9, bytes_accessed=40 * 2**20, transcendentals=0),
        name="update",
    )(label, left, gathered, front_entries, first, middle)

    step_rows = kept // 2
    schur = pl.pallas_call(
        functools.partial(finish_kernel, pivots),
        grid=(kept // step_rows,),
        out_shape=jax.ShapeDtypeStruct((1, kept, grp_total * kept), jnp.bfloat16),
        in_specs=[
            smem,
            smem,
            smem,
            whole(*rest.shape),
            pl.BlockSpec((grp_total, step_rows, 2 * LANE), lambda i: (0, i, 0)),
            pl.BlockSpec((grp_total, step_rows, rest_cols), lambda i: (0, i, 0)),
        ],
        out_specs=pl.BlockSpec((1, step_rows, grp_total * kept), lambda i: (0, i, 0)),
        scratch_shapes=[pltpu.VMEM((grp_total, step_rows, rest_cols), jnp.float32)],
        compiler_params=params(),
        cost_estimate=pl.CostEstimate(flops=10**7, bytes_accessed=30 * 2**20, transcendentals=0),
        name="finish",
    )(*lists, rest, done, open_)
    return schur, factors


def solution(mesh):
    placed = (
        P("front", "grp", None),
        P(("front", "grp"), None, None),
        P(("front", "grp"), None),
        P(("front", "grp")),
        P(("front", "grp")),
        P("front", None, None, None),
    )
    return jax.shard_map(
        local,
        mesh=mesh,
        in_specs=placed,
        out_specs=(P("front", "grp", None), P("front", None, "grp", None)),
        check_vma=False,
    )
```

```python
import functools

import jax
import jax.numpy as jnp
from jax import lax
from jax.experimental import pallas as pl
from jax.experimental.pallas import tpu as pltpu
from jax.sharding import PartitionSpec as P

LANE = 128
ROWTILE = 16
LABELROWS = 8
MIB = 1024 * 1024
NT = (((1,), (1,)), ((), ()))
NN = (((1,), (0,)), ((), ()))


def params(mebibytes=56):
    return pltpu.CompilerParams(vmem_limit_bytes=mebibytes * MIB)


def split(x):
    high = x.astype(jnp.bfloat16)
    return high, (x - high.astype(jnp.float32)).astype(jnp.bfloat16)


def dot_nt(a, b, form=NT):
    return lax.dot_general(a, b, form, preferred_element_type=jnp.float32)


def dot3(a, b, form=NT):
    a_high, a_low = a
    b_high, b_low = b
    return dot_nt(a_high, b_high, form) + (
        dot_nt(a_high, b_low, form) + dot_nt(a_low, b_high, form)
    )


def split_code(code):
    return split(code.astype(jnp.int32).astype(jnp.float32))


def encode(x):
    rows = x.shape[0]
    largest = jnp.max(jnp.abs(x), axis=1, keepdims=True)
    exponent = jnp.ceil(jnp.log2(jnp.clip(largest, 1e-30, 1e38)))
    scaled = jnp.round(x * jnp.exp2(15.0 - exponent))
    code = jnp.clip(scaled, -32767.0, 32767.0).astype(jnp.int32).astype(jnp.int16)
    along = jnp.transpose(jnp.broadcast_to(exponent, (rows, LANE)))[:ROWTILE]
    return code, along.astype(jnp.int32)


def scale_of(exponent):
    return jnp.exp2(exponent.astype(jnp.int32).astype(jnp.float32) - 15.0)


def pack_first_kernel(count, target, tile, blocks, out, position, load, marks, sem):
    devices = out.shape[0]
    slots, rows, _ = blocks.shape
    copy = pltpu.make_async_copy(blocks.at[:, :, pl.ds(0, LANE)], load, sem)
    copy.start()

    @pl.loop(0, devices, unroll=8)
    def _(t):
        marks[2, t] = 2 * t
        marks[0, t] = 0
        marks[1, t] = 0

    @pl.loop(0, slots, unroll=4)
    def _(i):
        t = target[i]
        at = marks[2, t]
        marks[2, t] = at + 1
        position[i] = at
        marks[at % 2, t] = jnp.where(i < count[0], tile[i] + 1, 0)

    row = lax.broadcasted_iota(jnp.int32, (LABELROWS, LANE), 0)

    @pl.loop(0, devices, unroll=8)
    def _(t):
        both = jnp.where(row == 0, marks[0, t], jnp.where(row == 1, marks[1, t], 0))
        out[t, 2 * rows :, :] = both.astype(jnp.float32).astype(jnp.bfloat16)

    copy.wait()

    @pl.loop(0, slots, unroll=4)
    def _(i):
        at = position[i]
        out[at // 2, pl.ds(pl.multiple_of((at % 2) * rows, rows), rows), :] = load[i]


def pack_rest_kernel(position, blocks, front, middle, rest, entries, sem):
    groups = entries.shape[0]
    width = front.shape[2] // groups

    def copy(c):
        return pltpu.make_async_copy(
            front.at[0, :, pl.ds(c * width, LANE)], entries.at[c], sem.at[c]
        )

    for c in range(groups):
        copy(c).start()

    @pl.loop(0, blocks.shape[0], unroll=2)
    def _(i):
        at = position[i]
        middle[at] = blocks[i, :, LANE : 2 * LANE]
        rest[at] = blocks[i, :, 2 * LANE :]

    for c in range(groups):
        copy(c).wait()


def gather_lanes(acc, rows, start, width, groups):
    per = LANE // width
    lane = lax.broadcasted_iota(jnp.int32, (rows, LANE), 1)
    out = []
    for tile in range(groups // per):
        total = None
        for k in range(per):
            piece = acc[tile * per + k, :rows]
            shift = (k * width - start) % LANE
            if shift:
                piece = pltpu.roll(piece, shift, 1)
            total = piece if total is None else jnp.where(lane >= k * width, piece, total)
        out.append(total)
    return jnp.concatenate(out, axis=1)


def list_blocks(label, groups, start, order, column, head, follow):
    sources = label.shape[1]

    @pl.loop(0, groups)
    def _(r):
        start[r] = 0
        head[r] = -1

    def each(act):
        @pl.loop(0, sources)
        def _(source):
            for k in range(2):
                at = label[k, source]

                @pl.when(at >= 0)
                def _():
                    act(2 * source + k, at // groups, at % groups)

    def count(slot, r, c):
        start[r] += 1
        follow[slot] = head[c]
        head[c] = slot

    def place(slot, r, c):
        at = start[r] - 1
        start[r] = at
        order[at] = slot
        column[at] = c

    each(count)
    start[groups] = 0

    @pl.loop(0, groups)
    def _(r):
        start[groups] += start[r]
        start[r] = start[groups]

    each(place)


def panel_kernel(
    pivots, arrived, entries, inverse, factor, second, code, label, start, order, column, head, follow,
    acc, marks, load, later, result, sem,
):
    groups, rows, _ = entries.shape
    sources = arrived.shape[0]
    block_rows = rows // groups
    dead = 2 * pivots
    inverse_copy = pltpu.make_async_copy(inverse.at[0, 0], load, sem.at[1])
    inverse_copy.start()

    shape = (sources, LABELROWS, LANE)
    own = lax.broadcasted_iota(jnp.int32, shape, 0) == lax.broadcasted_iota(jnp.int32, shape, 2)
    sent = arrived[:, 2 * block_rows :, :].astype(jnp.float32)
    label[...] = jnp.sum(jnp.where(own, sent, 0.0), axis=0).astype(jnp.int32) - 1
    copy = pltpu.make_async_copy(label, marks, sem.at[0])
    copy.start()
    acc[:, :rows] = entries[...].astype(jnp.float32)
    copy.wait()

    @pl.loop(0, sources, unroll=4)
    def _(source):
        for k in range(2):
            at = marks[k, source]
            at = jnp.where(at < 0, groups * groups, at)
            r, c = at // groups, at % groups
            where = pl.ds(pl.multiple_of(r * block_rows, block_rows), block_rows)
            block = arrived[source, k * block_rows : (k + 1) * block_rows, :]
            acc[c, where, :] += block.astype(jnp.float32)

    later[...] = gather_lanes(acc, rows, pivots, pivots, groups)
    later_copy = pltpu.make_async_copy(later, second, sem.at[2])
    later_copy.start()
    columns = gather_lanes(acc, rows, 0, pivots, groups)
    inverse_copy.wait()
    result[...] = dot3(split(columns), split(load[...]))
    result_copy = pltpu.make_async_copy(result, factor, sem.at[3])
    result_copy.start()
    codes, exponents = encode(result[...])
    later_codes, later_exponents = encode(later[...])
    kept, kept_later = rows - pivots, rows - dead
    code[:kept] = codes[pivots:]
    code[kept : kept + kept_later] = later_codes[dead:]
    row = lax.broadcasted_iota(jnp.int32, exponents.shape, 0)
    code[kept + kept_later :] = jnp.where(row == 0, exponents, later_exponents).astype(jnp.int16)
    list_blocks(marks, groups, start, order, column, head, follow)
    later_copy.wait()
    result_copy.wait()


def left_kernel(pivots, gathered, factor, second, inverse, factors, left, pivot_code, exponent, sem):
    groups, code_rows, _ = gathered.shape
    rows, panel = factor.shape
    copies = [
        pltpu.make_async_copy(gathered.at[:, pl.ds(0, pivots), :], pivot_code, sem.at[0]),
        pltpu.make_async_copy(
            gathered.at[:, pl.ds(code_rows - ROWTILE, ROWTILE), :], exponent, sem.at[1]
        ),
    ]
    for copy in copies:
        copy.start()
    factors[0, 0] = factor[...]
    for copy in copies:
        copy.wait()
    lane = lax.broadcasted_iota(jnp.int32, (ROWTILE, panel), 1)
    total = jnp.zeros((ROWTILE, panel), jnp.float32)
    for g in range(groups):
        scale = pltpu.roll(scale_of(exponent[g]), (g * pivots - pivots) % panel, 1)
        total = jnp.where((lane >= g * pivots) & (lane < (g + 1) * pivots), scale, total)
    scale = total[:1]
    pivot_rows = split_code(pivot_code[...].reshape(groups * pivots, panel))
    inverse_parts = split(inverse[0, 0])
    first = factor[pivots:]
    update = dot3(split(first), pivot_rows) * scale
    result = dot3(split(second[pivots:] - update), inverse_parts)
    factors[0, 1, :pivots] = jnp.zeros((pivots, panel), jnp.float32)
    factors[0, 1, pivots:] = result
    own = dot3(split(result[pivots:]), inverse_parts, NN)
    mixed = first[pivots:] - dot3(split(own * scale), pivot_rows, NN)
    for k, part in enumerate((mixed, own)):
        high, low = split(part)
        left[k, :, :panel] = high
        left[k, :, panel : 2 * panel] = high
        left[k, :, 2 * panel :] = low


def update_kernel(
    pivots, label, head, follow, left, code, front, first, middle, done, open_, right, acc
):
    rows, panel = right.shape[1], code.shape[2]
    groups = head.shape[0]
    block_rows = rows // groups
    dead = 2 * pivots
    step = pl.program_id(0)

    @pl.when(step == 0)
    def _():
        right[...] = jnp.zeros(right.shape, jnp.bfloat16)

    for d in range(2):
        acc[d] = front[0, :, d * rows : d * rows + 2 * LANE].astype(jnp.float32)

        def add(slot, d=d):
            k = slot % 2
            r = label[k, slot // 2] // groups
            where = pl.ds(pl.multiple_of(r * block_rows, block_rows), block_rows)
            source = pl.ds(pl.multiple_of(k * block_rows, block_rows), block_rows)
            acc[d, where, :LANE] += first[slot // 2, source, :].astype(jnp.float32)
            acc[d, where, LANE:] += middle[slot].astype(jnp.float32)
            return follow[slot]

        lax.while_loop(lambda slot: slot >= 0, add, head[2 * step + d])

    kept = (rows - pivots, rows - dead)
    starts = (0, kept[0])
    for d in range(2):
        scale = scale_of(code[d, kept[0] + kept[1] :])
        columns = slice(d * rows + 2 * LANE, (d + 1) * rows)
        total = jnp.concatenate(
            [acc[d, dead:], front[0, dead:, columns].astype(jnp.float32)], axis=1
        )
        for k in range(2):
            high, low = split_code(code[d, starts[k] : starts[k] + kept[k]])
            right[k, rows - kept[k] :, :panel] = high
            right[k, rows - kept[k] :, panel : 2 * panel] = low
            right[k, rows - kept[k] :, 2 * panel :] = high
            total = total - dot_nt(left[k], right[k]) * scale[k : k + 1]
        done[2 * step + d] = total[:, : 2 * LANE].astype(jnp.bfloat16)
        open_[2 * step + d] = total[:, 2 * LANE :]


def finish_kernel(pivots, start, order, column, rest, done, open_, out, acc):
    groups, step_rows, _ = acc.shape
    block_rows = rest.shape[1]
    dead = 2 * pivots
    kept = 4 * LANE - dead
    per = step_rows // block_rows
    row = pl.program_id(0) * per + groups - pl.num_programs(0) * per
    here = pl.ds(pl.multiple_of(pl.program_id(0) * step_rows, ROWTILE), step_rows)
    acc[...] = jnp.zeros(acc.shape, jnp.float32)
    for p in range(per):

        @pl.loop(start[row + p], start[row + p + 1])
        def _(i):
            block = rest[order[i]].astype(jnp.float32)
            acc[column[i], p * block_rows : (p + 1) * block_rows, :] += block

    for m in range(groups // 2):
        sides = []
        for c in (2 * m, 2 * m + 1):
            sides.append(done[c, here, dead:])
            sides.append((open_[c, here] + acc[c]).astype(jnp.bfloat16))
        pair = jnp.concatenate(sides, axis=1)
        out[0, :, 2 * m * kept : 2 * (m + 1) * kept] = pair


def local(front_entries, child_blocks, dest_device, dest_tile, child_count, diag_inverse):
    grp_total = lax.axis_size("grp")
    device_total = grp_total * lax.axis_size("front")
    axes = ("front", "grp")
    slots, block_rows, block_cols = child_blocks.shape
    _, rows, width = front_entries.shape
    panel = diag_inverse.shape[2]
    pivots = panel // grp_total
    slot_count = 2 * device_total
    rest_cols = block_cols - 2 * LANE
    hbm = pl.BlockSpec(memory_space=pl.ANY)
    vmem = pl.BlockSpec(memory_space=pltpu.VMEM)
    smem = pl.BlockSpec(memory_space=pltpu.SMEM)
    whole = lambda *shape: pl.BlockSpec(shape, lambda i: (0,) * len(shape))

    first_rows = 2 * block_rows + LABELROWS
    first_out, position = pl.pallas_call(
        pack_first_kernel,
        grid=(1,),
        out_shape=(
            pltpu.VMEM((device_total, first_rows, LANE), jnp.bfloat16),
            jax.ShapeDtypeStruct((slots,), jnp.int32),
        ),
        in_specs=[smem, smem, smem, hbm],
        out_specs=(vmem, smem),
        scratch_shapes=[
            pltpu.VMEM((slots, block_rows, LANE), jnp.bfloat16),
            pltpu.SMEM((3, device_total), jnp.int32),
            pltpu.SemaphoreType.DMA,
        ],
        compiler_params=params(),
        name="pack_first",
    )(child_count, dest_device.reshape(slots), dest_tile, child_blocks)
    first = lax.all_to_all(first_out, axes, split_axis=0, concat_axis=0, tiled=True)
    middle_out, rest_out, entries = pl.pallas_call(
        pack_rest_kernel,
        grid=(1,),
        out_shape=(
            jax.ShapeDtypeStruct((slot_count, block_rows, LANE), jnp.bfloat16),
            jax.ShapeDtypeStruct((slot_count, block_rows, rest_cols), jnp.bfloat16),
            jax.ShapeDtypeStruct((grp_total, rows, LANE), jnp.bfloat16),
        ),
        in_specs=[smem, whole(*child_blocks.shape), hbm],
        out_specs=(
            whole(slot_count, block_rows, LANE),
            whole(slot_count, block_rows, rest_cols),
            whole(grp_total, rows, LANE),
        ),
        scratch_shapes=[pltpu.SemaphoreType.DMA((grp_total,))],
        compiler_params=params(),
        cost_estimate=pl.CostEstimate(flops=0, bytes_accessed=16 * 2**20, transcendentals=0),
        name="pack_rest",
    )(position, child_blocks, front_entries)
    middle = lax.all_to_all(middle_out, axes, split_axis=0, concat_axis=0, tiled=True)
    first, rest_out, entries = lax.optimization_barrier((first, rest_out, entries))

    kept = rows - 2 * pivots
    code_rows = (rows - pivots) + kept + ROWTILE
    inverse_spec = lambda k: pl.BlockSpec((1, 1, panel, panel), lambda i: (0, k, 0, 0))
    row_blocks = rows // block_rows
    lengths = (row_blocks + 1, slot_count, slot_count, row_blocks, slot_count)
    factor, second, code, label, start, order, column, head, follow = pl.pallas_call(
        functools.partial(panel_kernel, pivots),
        grid=(1,),
        out_shape=(
            jax.ShapeDtypeStruct((rows, panel), jnp.float32),
            jax.ShapeDtypeStruct((rows, panel), jnp.float32),
            jax.ShapeDtypeStruct((code_rows, panel), jnp.int16),
            jax.ShapeDtypeStruct((LABELROWS, LANE), jnp.int32),
            *(jax.ShapeDtypeStruct((length,), jnp.int32) for length in lengths),
        ),
        in_specs=[whole(*first.shape), whole(*entries.shape), hbm],
        out_specs=(hbm, hbm, whole(code_rows, panel), whole(LABELROWS, LANE)) + (smem,) * 5,
        scratch_shapes=[
            pltpu.VMEM((grp_total, rows + block_rows, LANE), jnp.float32),
            pltpu.SMEM((LABELROWS, LANE), jnp.int32),
            pltpu.VMEM((panel, panel), jnp.float32),
            pltpu.VMEM((rows, panel), jnp.float32),
            pltpu.VMEM((rows, panel), jnp.float32),
            pltpu.SemaphoreType.DMA((4,)),
        ],
        compiler_params=params(),
        cost_estimate=pl.CostEstimate(flops=2 * 10**9, bytes_accessed=10 * 2**20, transcendentals=0),
        name="panels",
    )(first, entries, diag_inverse)
    gathered = lax.all_gather(code, "grp", axis=0, tiled=False)

    gathered, rest_out = lax.optimization_barrier((gathered, rest_out))
    rest = lax.all_to_all(rest_out, axes, split_axis=0, concat_axis=0, tiled=True)

    factors, left = pl.pallas_call(
        functools.partial(left_kernel, pivots),
        grid=(1,),
        out_shape=(
            jax.ShapeDtypeStruct((1, 2, rows, panel), jnp.float32),
            jax.ShapeDtypeStruct((2, kept, 3 * panel), jnp.bfloat16),
        ),
        in_specs=[hbm, whole(rows, panel), whole(rows, panel), inverse_spec(1)],
        out_specs=(whole(1, 2, rows, panel), whole(2, kept, 3 * panel)),
        scratch_shapes=[
            pltpu.VMEM((grp_total, pivots, panel), jnp.int16),
            pltpu.VMEM((grp_total, ROWTILE, panel), jnp.int16),
            pltpu.SemaphoreType.DMA((2,)),
        ],
        compiler_params=params(),
        cost_estimate=pl.CostEstimate(flops=4 * 10**9, bytes_accessed=8 * 2**20, transcendentals=0),
        name="left_factors",
    )(gathered, factor, second, diag_inverse)

    done, open_ = pl.pallas_call(
        functools.partial(update_kernel, pivots),
        grid=(grp_total // 2,),
        out_shape=(
            pltpu.VMEM((grp_total, kept, 2 * LANE), jnp.bfloat16),
            pltpu.VMEM((grp_total, kept, rest_cols), jnp.float32),
        ),
        in_specs=[
            smem,
            smem,
            smem,
            whole(2, kept, 3 * panel),
            pl.BlockSpec((2, code_rows, panel), lambda i: (i, 0, 0)),
            pl.BlockSpec((1, rows, 2 * rows), lambda i: (0, 0, i)),
            whole(*first.shape),
            whole(*middle.shape),
        ],
        out_specs=(vmem, vmem),
        scratch_shapes=[
            pltpu.VMEM((2, rows, 3 * panel), jnp.bfloat16),
            pltpu.VMEM((2, rows, 2 * LANE), jnp.float32),
        ],
        compiler_params=params(52),
        cost_estimate=pl.CostEstimate(flops=20 * 10**9, bytes_accessed=40 * 2**20, transcendentals=0),
        name="update",
    )(label, head, follow, left, gathered, front_entries, first, middle)

    step_rows = kept // 2
    done, open_ = (pltpu.with_memory_space_constraint(x, pltpu.VMEM) for x in (done, open_))
    schur = pl.pallas_call(
        functools.partial(finish_kernel, pivots),
        grid=(kept // step_rows,),
        out_shape=jax.ShapeDtypeStruct((1, kept, grp_total * kept), jnp.bfloat16),
        in_specs=[
            smem,
            smem,
            smem,
            whole(*rest.shape),
            vmem,
            vmem,
        ],
        out_specs=pl.BlockSpec((1, step_rows, grp_total * kept), lambda i: (0, i, 0)),
        scratch_shapes=[pltpu.VMEM((grp_total, step_rows, rest_cols), jnp.float32)],
        compiler_params=params(52),
        cost_estimate=pl.CostEstimate(flops=10**7, bytes_accessed=30 * 2**20, transcendentals=0),
        name="finish",
    )(start, order, column, rest, done, open_)
    return schur, factors


def solution(mesh):
    placed = (
        P("front", "grp", None),
        P(("front", "grp"), None, None),
        P(("front", "grp"), None),
        P(("front", "grp")),
        P(("front", "grp")),
        P("front", None, None, None),
    )
    return jax.shard_map(
        local,
        mesh=mesh,
        in_specs=placed,
        out_specs=(P("front", "grp", None), P("front", None, "grp", None)),
        check_vma=False,
    )
```

```python
import functools

import jax
import jax.numpy as jnp
from jax import lax
from jax.experimental import pallas as pl
from jax.experimental.pallas import tpu as pltpu
from jax.sharding import PartitionSpec as P

LANE = 128
ROWTILE = 16
LABELROWS = 8
MIB = 1024 * 1024
NT = (((1,), (1,)), ((), ()))
NN = (((1,), (0,)), ((), ()))


def params(mebibytes=56):
    return pltpu.CompilerParams(vmem_limit_bytes=mebibytes * MIB)


def split(x):
    high = x.astype(jnp.bfloat16)
    return high, (x - high.astype(jnp.float32)).astype(jnp.bfloat16)


def dot_nt(a, b, form=NT):
    return lax.dot_general(a, b, form, preferred_element_type=jnp.float32)


def dot3(a, b, form=NT):
    a_high, a_low = a
    b_high, b_low = b
    return dot_nt(a_high, b_high, form) + (
        dot_nt(a_high, b_low, form) + dot_nt(a_low, b_high, form)
    )


def split_code(code):
    return split(code.astype(jnp.int32).astype(jnp.float32))


def encode(x):
    rows = x.shape[0]
    largest = jnp.max(jnp.abs(x), axis=1, keepdims=True)
    exponent = jnp.ceil(jnp.log2(jnp.clip(largest, 1e-30, 1e38)))
    scaled = jnp.round(x * jnp.exp2(15.0 - exponent))
    code = jnp.clip(scaled, -32767.0, 32767.0).astype(jnp.int32).astype(jnp.int16)
    along = jnp.transpose(jnp.broadcast_to(exponent, (rows, LANE)))[:ROWTILE]
    return code, along.astype(jnp.int32)


def scale_of(exponent):
    return jnp.exp2(exponent.astype(jnp.int32).astype(jnp.float32) - 15.0)


def pack_first_kernel(count, target, tile, blocks, out, position, load, marks, sem):
    devices = out.shape[0]
    slots, rows, _ = blocks.shape
    copy = pltpu.make_async_copy(blocks.at[:, :, pl.ds(0, LANE)], load, sem)
    copy.start()

    @pl.loop(0, devices, unroll=8)
    def _(t):
        marks[2, t] = 2 * t
        marks[0, t] = 0
        marks[1, t] = 0

    @pl.loop(0, slots, unroll=4)
    def _(i):
        t = target[i]
        at = marks[2, t]
        marks[2, t] = at + 1
        position[i] = at
        marks[at % 2, t] = jnp.where(i < count[0], tile[i] + 1, 0)

    row = lax.broadcasted_iota(jnp.int32, (LABELROWS, LANE), 0)

    @pl.loop(0, devices, unroll=8)
    def _(t):
        both = jnp.where(row == 0, marks[0, t], jnp.where(row == 1, marks[1, t], 0))
        out[t, 2 * rows :, :] = both.astype(jnp.float32).astype(jnp.bfloat16)

    copy.wait()

    @pl.loop(0, slots, unroll=4)
    def _(i):
        at = position[i]
        out[at // 2, pl.ds(pl.multiple_of((at % 2) * rows, rows), rows), :] = load[i]


def pack_rest_kernel(position, blocks, front, middle, rest, entries, sem):
    groups = entries.shape[0]
    width = front.shape[2] // groups

    def copy(c):
        return pltpu.make_async_copy(
            front.at[0, :, pl.ds(c * width, LANE)], entries.at[c], sem.at[c]
        )

    for c in range(groups):
        copy(c).start()

    @pl.loop(0, blocks.shape[0], unroll=2)
    def _(i):
        at = position[i]
        middle[at] = blocks[i, :, LANE : 2 * LANE]
        rest[at] = blocks[i, :, 2 * LANE :]

    for c in range(groups):
        copy(c).wait()


def gather_lanes(acc, rows, start, width, groups):
    per = LANE // width
    lane = lax.broadcasted_iota(jnp.int32, (rows, LANE), 1)
    out = []
    for tile in range(groups // per):
        total = None
        for k in range(per):
            piece = acc[tile * per + k, :rows]
            shift = (k * width - start) % LANE
            if shift:
                piece = pltpu.roll(piece, shift, 1)
            total = piece if total is None else jnp.where(lane >= k * width, piece, total)
        out.append(total)
    return jnp.concatenate(out, axis=1)


def list_blocks(label, groups, start, order, column, head, follow):
    sources = label.shape[1]

    @pl.loop(0, groups)
    def _(r):
        start[r] = 0
        head[r] = -1

    def each(act):
        @pl.loop(0, sources)
        def _(source):
            for k in range(2):
                at = label[k, source]

                @pl.when(at >= 0)
                def _():
                    act(2 * source + k, at // groups, at % groups)

    def count(slot, r, c):
        start[r] += 1
        follow[slot] = head[c]
        head[c] = slot

    def place(slot, r, c):
        at = start[r] - 1
        start[r] = at
        order[at] = slot
        column[at] = c

    each(count)
    start[groups] = 0

    @pl.loop(0, groups)
    def _(r):
        start[groups] += start[r]
        start[r] = start[groups]

    each(place)


def panel_kernel(
    pivots, arrived, entries, inverse, factor, second, code, label, start, order, column, head, follow,
    acc, marks, load, later, result, sem,
):
    groups, rows, _ = entries.shape
    sources = arrived.shape[0]
    block_rows = rows // groups
    dead = 2 * pivots
    inverse_copy = pltpu.make_async_copy(inverse.at[0, 0], load, sem.at[1])
    inverse_copy.start()

    shape = (sources, LABELROWS, LANE)
    own = lax.broadcasted_iota(jnp.int32, shape, 0) == lax.broadcasted_iota(jnp.int32, shape, 2)
    sent = arrived[:, 2 * block_rows :, :].astype(jnp.float32)
    label[...] = jnp.sum(jnp.where(own, sent, 0.0), axis=0).astype(jnp.int32) - 1
    copy = pltpu.make_async_copy(label, marks, sem.at[0])
    copy.start()
    acc[:, :rows] = entries[...].astype(jnp.float32)
    copy.wait()

    @pl.loop(0, sources, unroll=4)
    def _(source):
        for k in range(2):
            at = marks[k, source]
            at = jnp.where(at < 0, groups * groups, at)
            r, c = at // groups, at % groups
            where = pl.ds(pl.multiple_of(r * block_rows, block_rows), block_rows)
            block = arrived[source, k * block_rows : (k + 1) * block_rows, :]
            acc[c, where, :] += block.astype(jnp.float32)

    later[...] = gather_lanes(acc, rows, pivots, pivots, groups)
    later_copy = pltpu.make_async_copy(later, second, sem.at[2])
    later_copy.start()
    columns = gather_lanes(acc, rows, 0, pivots, groups)
    inverse_copy.wait()
    result[...] = dot3(split(columns), split(load[...]))
    result_copy = pltpu.make_async_copy(result, factor, sem.at[3])
    result_copy.start()
    codes, exponents = encode(result[...])
    later_codes, later_exponents = encode(later[...])
    kept, kept_later = rows - pivots, rows - dead
    code[:kept] = codes[pivots:]
    code[kept : kept + kept_later] = later_codes[dead:]
    row = lax.broadcasted_iota(jnp.int32, exponents.shape, 0)
    code[kept + kept_later :] = jnp.where(row == 0, exponents, later_exponents).astype(jnp.int16)
    list_blocks(marks, groups, start, order, column, head, follow)
    later_copy.wait()
    result_copy.wait()


def left_kernel(pivots, gathered, factor, second, inverse, factors, left, pivot_code, exponent, sem):
    groups, code_rows, _ = gathered.shape
    rows, panel = factor.shape
    copies = [
        pltpu.make_async_copy(gathered.at[:, pl.ds(0, pivots), :], pivot_code, sem.at[0]),
        pltpu.make_async_copy(
            gathered.at[:, pl.ds(code_rows - ROWTILE, ROWTILE), :], exponent, sem.at[1]
        ),
    ]
    for copy in copies:
        copy.start()
    factors[0, 0] = factor[...]
    for copy in copies:
        copy.wait()
    lane = lax.broadcasted_iota(jnp.int32, (ROWTILE, panel), 1)
    total = jnp.zeros((ROWTILE, panel), jnp.float32)
    for g in range(groups):
        scale = pltpu.roll(scale_of(exponent[g]), (g * pivots - pivots) % panel, 1)
        total = jnp.where((lane >= g * pivots) & (lane < (g + 1) * pivots), scale, total)
    scale = total[:1]
    pivot_rows = split_code(pivot_code[...].reshape(groups * pivots, panel))
    inverse_parts = split(inverse[0, 0])
    first = factor[pivots:]
    update = dot3(split(first), pivot_rows) * scale
    result = dot3(split(second[pivots:] - update), inverse_parts)
    factors[0, 1, :pivots] = jnp.zeros((pivots, panel), jnp.float32)
    factors[0, 1, pivots:] = result
    own = dot3(split(result[pivots:]), inverse_parts, NN)
    mixed = first[pivots:] - dot3(split(own * scale), pivot_rows, NN)
    for k, part in enumerate((mixed, own)):
        high, low = split(part)
        left[k, :, :panel] = high
        left[k, :, panel : 2 * panel] = high
        left[k, :, 2 * panel :] = low


def update_kernel(
    pivots, label, head, follow, left, code, front, first, middle, done, open_, right, acc
):
    rows, panel = right.shape[1], code.shape[2]
    groups = head.shape[0]
    block_rows = rows // groups
    dead = 2 * pivots
    step = pl.program_id(0)

    @pl.when(step == 0)
    def _():
        right[...] = jnp.zeros(right.shape, jnp.bfloat16)

    for d in range(2):
        acc[d] = front[0, :, d * rows : d * rows + 2 * LANE].astype(jnp.float32)

        def add(slot, d=d):
            k = slot % 2
            r = label[k, slot // 2] // groups
            where = pl.ds(pl.multiple_of(r * block_rows, block_rows), block_rows)
            source = pl.ds(pl.multiple_of(k * block_rows, block_rows), block_rows)
            acc[d, where, :LANE] += first[slot // 2, source, :].astype(jnp.float32)
            acc[d, where, LANE:] += middle[slot].astype(jnp.float32)
            return follow[slot]

        lax.while_loop(lambda slot: slot >= 0, add, head[2 * step + d])

    kept = (rows - pivots, rows - dead)
    starts = (0, kept[0])
    for d in range(2):
        scale = scale_of(code[d, kept[0] + kept[1] :])
        columns = slice(d * rows + 2 * LANE, (d + 1) * rows)
        total = jnp.concatenate(
            [acc[d, dead:], front[0, dead:, columns].astype(jnp.float32)], axis=1
        )
        for k in range(2):
            high, low = split_code(code[d, starts[k] : starts[k] + kept[k]])
            right[k, rows - kept[k] :, :panel] = high
            right[k, rows - kept[k] :, panel : 2 * panel] = low
            right[k, rows - kept[k] :, 2 * panel :] = high
            total = total - dot_nt(left[k], right[k]) * scale[k : k + 1]
        done[d] = total[:, : 2 * LANE].astype(jnp.bfloat16)
        open_[d] = total[:, 2 * LANE :]


def finish_kernel(pivots, start, order, column, rest, done, open_, out, acc):
    groups, step_rows, _ = acc.shape
    block_rows = rest.shape[1]
    dead = 2 * pivots
    kept = 4 * LANE - dead
    per = step_rows // block_rows
    row = pl.program_id(0) * per + groups - pl.num_programs(0) * per
    acc[...] = jnp.zeros(acc.shape, jnp.float32)
    for p in range(per):

        @pl.loop(start[row + p], start[row + p + 1])
        def _(i):
            block = rest[order[i]].astype(jnp.float32)
            acc[column[i], p * block_rows : (p + 1) * block_rows, :] += block

    for m in range(groups // 2):
        sides = []
        for c in (2 * m, 2 * m + 1):
            sides.append(done[c, :, dead:])
            sides.append((open_[c] + acc[c]).astype(jnp.bfloat16))
        pair = jnp.concatenate(sides, axis=1)
        out[0, :, 2 * m * kept : 2 * (m + 1) * kept] = pair


def local(front_entries, child_blocks, dest_device, dest_tile, child_count, diag_inverse):
    grp_total = lax.axis_size("grp")
    device_total = grp_total * lax.axis_size("front")
    axes = ("front", "grp")
    slots, block_rows, block_cols = child_blocks.shape
    _, rows, width = front_entries.shape
    panel = diag_inverse.shape[2]
    pivots = panel // grp_total
    slot_count = 2 * device_total
    rest_cols = block_cols - 2 * LANE
    hbm = pl.BlockSpec(memory_space=pl.ANY)
    smem = pl.BlockSpec(memory_space=pltpu.SMEM)
    whole = lambda *shape: pl.BlockSpec(shape, lambda i: (0,) * len(shape))

    first_rows = 2 * block_rows + LABELROWS
    first_out, position = pl.pallas_call(
        pack_first_kernel,
        grid=(1,),
        out_shape=(
            jax.ShapeDtypeStruct((device_total, first_rows, LANE), jnp.bfloat16),
            jax.ShapeDtypeStruct((slots,), jnp.int32),
        ),
        in_specs=[smem, smem, smem, hbm],
        out_specs=(whole(device_total, first_rows, LANE), smem),
        scratch_shapes=[
            pltpu.VMEM((slots, block_rows, LANE), jnp.bfloat16),
            pltpu.SMEM((3, device_total), jnp.int32),
            pltpu.SemaphoreType.DMA,
        ],
        compiler_params=params(),
        name="pack_first",
    )(child_count, dest_device.reshape(slots), dest_tile, child_blocks)
    first = lax.all_to_all(first_out, axes, split_axis=0, concat_axis=0, tiled=True)
    middle_out, rest_out, entries = pl.pallas_call(
        pack_rest_kernel,
        grid=(1,),
        out_shape=(
            jax.ShapeDtypeStruct((slot_count, block_rows, LANE), jnp.bfloat16),
            jax.ShapeDtypeStruct((slot_count, block_rows, rest_cols), jnp.bfloat16),
            jax.ShapeDtypeStruct((grp_total, rows, LANE), jnp.bfloat16),
        ),
        in_specs=[smem, whole(*child_blocks.shape), hbm],
        out_specs=(
            whole(slot_count, block_rows, LANE),
            whole(slot_count, block_rows, rest_cols),
            whole(grp_total, rows, LANE),
        ),
        scratch_shapes=[pltpu.SemaphoreType.DMA((grp_total,))],
        compiler_params=params(),
        cost_estimate=pl.CostEstimate(flops=0, bytes_accessed=16 * 2**20, transcendentals=0),
        name="pack_rest",
    )(position, child_blocks, front_entries)
    middle = lax.all_to_all(middle_out, axes, split_axis=0, concat_axis=0, tiled=True)
    first, rest_out, entries = lax.optimization_barrier((first, rest_out, entries))

    kept = rows - 2 * pivots
    code_rows = (rows - pivots) + kept + ROWTILE
    inverse_spec = lambda k: pl.BlockSpec((1, 1, panel, panel), lambda i: (0, k, 0, 0))
    row_blocks = rows // block_rows
    lengths = (row_blocks + 1, slot_count, slot_count, row_blocks, slot_count)
    factor, second, code, label, start, order, column, head, follow = pl.pallas_call(
        functools.partial(panel_kernel, pivots),
        grid=(1,),
        out_shape=(
            jax.ShapeDtypeStruct((rows, panel), jnp.float32),
            jax.ShapeDtypeStruct((rows, panel), jnp.float32),
            jax.ShapeDtypeStruct((code_rows, panel), jnp.int16),
            jax.ShapeDtypeStruct((LABELROWS, LANE), jnp.int32),
            *(jax.ShapeDtypeStruct((length,), jnp.int32) for length in lengths),
        ),
        in_specs=[whole(*first.shape), whole(*entries.shape), hbm],
        out_specs=(hbm, hbm, whole(code_rows, panel), whole(LABELROWS, LANE)) + (smem,) * 5,
        scratch_shapes=[
            pltpu.VMEM((grp_total, rows + block_rows, LANE), jnp.float32),
            pltpu.SMEM((LABELROWS, LANE), jnp.int32),
            pltpu.VMEM((panel, panel), jnp.float32),
            pltpu.VMEM((rows, panel), jnp.float32),
            pltpu.VMEM((rows, panel), jnp.float32),
            pltpu.SemaphoreType.DMA((4,)),
        ],
        compiler_params=params(),
        cost_estimate=pl.CostEstimate(flops=2 * 10**9, bytes_accessed=10 * 2**20, transcendentals=0),
        name="panels",
    )(first, entries, diag_inverse)
    gathered = lax.all_gather(code, "grp", axis=0, tiled=False)

    gathered, rest_out = lax.optimization_barrier((gathered, rest_out))
    rest = lax.all_to_all(rest_out, axes, split_axis=0, concat_axis=0, tiled=True)

    factors, left = pl.pallas_call(
        functools.partial(left_kernel, pivots),
        grid=(1,),
        out_shape=(
            jax.ShapeDtypeStruct((1, 2, rows, panel), jnp.float32),
            jax.ShapeDtypeStruct((2, kept, 3 * panel), jnp.bfloat16),
        ),
        in_specs=[hbm, whole(rows, panel), whole(rows, panel), inverse_spec(1)],
        out_specs=(whole(1, 2, rows, panel), whole(2, kept, 3 * panel)),
        scratch_shapes=[
            pltpu.VMEM((grp_total, pivots, panel), jnp.int16),
            pltpu.VMEM((grp_total, ROWTILE, panel), jnp.int16),
            pltpu.SemaphoreType.DMA((2,)),
        ],
        compiler_params=params(),
        cost_estimate=pl.CostEstimate(flops=4 * 10**9, bytes_accessed=8 * 2**20, transcendentals=0),
        name="left_factors",
    )(gathered, factor, second, diag_inverse)

    done, open_ = pl.pallas_call(
        functools.partial(update_kernel, pivots),
        grid=(grp_total // 2,),
        out_shape=(
            jax.ShapeDtypeStruct((grp_total, kept, 2 * LANE), jnp.bfloat16),
            jax.ShapeDtypeStruct((grp_total, kept, rest_cols), jnp.float32),
        ),
        in_specs=[
            smem,
            smem,
            smem,
            whole(2, kept, 3 * panel),
            pl.BlockSpec((2, code_rows, panel), lambda i: (i, 0, 0)),
            pl.BlockSpec((1, rows, 2 * rows), lambda i: (0, 0, i)),
            whole(*first.shape),
            whole(*middle.shape),
        ],
        out_specs=(
            pl.BlockSpec((2, kept, 2 * LANE), lambda i: (i, 0, 0)),
            pl.BlockSpec((2, kept, rest_cols), lambda i: (i, 0, 0)),
        ),
        scratch_shapes=[
            pltpu.VMEM((2, rows, 3 * panel), jnp.bfloat16),
            pltpu.VMEM((2, rows, 2 * LANE), jnp.float32),
        ],
        compiler_params=params(),
        cost_estimate=pl.CostEstimate(flops=20 * 10**9, bytes_accessed=40 * 2**20, transcendentals=0),
        name="update",
    )(label, head, follow, left, gathered, front_entries, first, middle)

    step_rows = kept // 2
    schur = pl.pallas_call(
        functools.partial(finish_kernel, pivots),
        grid=(kept // step_rows,),
        out_shape=jax.ShapeDtypeStruct((1, kept, grp_total * kept), jnp.bfloat16),
        in_specs=[
            smem,
            smem,
            smem,
            whole(*rest.shape),
            pl.BlockSpec((grp_total, step_rows, 2 * LANE), lambda i: (0, i, 0)),
            pl.BlockSpec((grp_total, step_rows, rest_cols), lambda i: (0, i, 0)),
        ],
        out_specs=pl.BlockSpec((1, step_rows, grp_total * kept), lambda i: (0, i, 0)),
        scratch_shapes=[pltpu.VMEM((grp_total, step_rows, rest_cols), jnp.float32)],
        compiler_params=params(),
        cost_estimate=pl.CostEstimate(flops=10**7, bytes_accessed=30 * 2**20, transcendentals=0),
        name="finish",
    )(start, order, column, rest, done, open_)
    return schur, factors


def solution(mesh):
    placed = (
        P("front", "grp", None),
        P(("front", "grp"), None, None),
        P(("front", "grp"), None),
        P(("front", "grp")),
        P(("front", "grp")),
        P("front", None, None, None),
    )
    return jax.shard_map(
        local,
        mesh=mesh,
        in_specs=placed,
        out_specs=(P("front", "grp", None), P("front", None, "grp", None)),
        check_vma=False,
    )
```

```python
import functools

import jax
import jax.numpy as jnp
from jax import lax
from jax.experimental import pallas as pl
from jax.experimental.pallas import tpu as pltpu
from jax.sharding import PartitionSpec as P

LANE = 128
ROWTILE = 16
LABELROWS = 8
MIB = 1024 * 1024
NT = (((1,), (1,)), ((), ()))
NN = (((1,), (0,)), ((), ()))


def params(mebibytes=56):
    return pltpu.CompilerParams(vmem_limit_bytes=mebibytes * MIB)


def split(x):
    high = x.astype(jnp.bfloat16)
    return high, (x - high.astype(jnp.float32)).astype(jnp.bfloat16)


def dot_nt(a, b, form=NT):
    return lax.dot_general(a, b, form, preferred_element_type=jnp.float32)


def dot3(a, b, form=NT):
    a_high, a_low = a
    b_high, b_low = b
    return dot_nt(a_high, b_high, form) + (
        dot_nt(a_high, b_low, form) + dot_nt(a_low, b_high, form)
    )


def split_code(code):
    return split(code.astype(jnp.int32).astype(jnp.float32))


def encode(x):
    rows = x.shape[0]
    largest = jnp.max(jnp.abs(x), axis=1, keepdims=True)
    exponent = jnp.ceil(jnp.log2(jnp.clip(largest, 1e-30, 1e38)))
    scaled = jnp.round(x * jnp.exp2(15.0 - exponent))
    code = jnp.clip(scaled, -32767.0, 32767.0).astype(jnp.int32).astype(jnp.int16)
    along = jnp.transpose(jnp.broadcast_to(exponent, (rows, LANE)))[:ROWTILE]
    return code, along.astype(jnp.int32)


def scale_of(exponent):
    return jnp.exp2(exponent.astype(jnp.int32).astype(jnp.float32) - 15.0)


def pack_first_kernel(count, target, tile, blocks, out, position, load, marks, sem):
    devices = out.shape[0]
    slots, rows, _ = blocks.shape
    copy = pltpu.make_async_copy(blocks.at[:, :, pl.ds(0, LANE)], load, sem)
    copy.start()

    @pl.loop(0, devices, unroll=8)
    def _(t):
        marks[2, t] = 2 * t
        marks[0, t] = 0
        marks[1, t] = 0

    @pl.loop(0, slots, unroll=4)
    def _(i):
        t = target[i]
        at = marks[2, t]
        marks[2, t] = at + 1
        position[i] = at
        marks[at % 2, t] = jnp.where(i < count[0], tile[i] + 1, 0)

    row = lax.broadcasted_iota(jnp.int32, (LABELROWS, LANE), 0)

    @pl.loop(0, devices, unroll=8)
    def _(t):
        both = jnp.where(row == 0, marks[0, t], jnp.where(row == 1, marks[1, t], 0))
        out[t, 2 * rows :, :] = both.astype(jnp.float32).astype(jnp.bfloat16)

    copy.wait()

    @pl.loop(0, slots, unroll=4)
    def _(i):
        at = position[i]
        out[at // 2, pl.ds(pl.multiple_of((at % 2) * rows, rows), rows), :] = load[i]


def pack_rest_kernel(position, blocks, front, middle, rest, entries, sem):
    groups = entries.shape[0]
    width = front.shape[2] // groups

    def copy(c):
        return pltpu.make_async_copy(
            front.at[0, :, pl.ds(c * width, LANE)], entries.at[c], sem.at[c]
        )

    for c in range(groups):
        copy(c).start()

    @pl.loop(0, blocks.shape[0], unroll=2)
    def _(i):
        at = position[i]
        middle[at] = blocks[i, :, LANE : 2 * LANE]
        rest[at] = blocks[i, :, 2 * LANE :]

    for c in range(groups):
        copy(c).wait()


def gather_lanes(acc, rows, start, width, groups):
    per = LANE // width
    lane = lax.broadcasted_iota(jnp.int32, (rows, LANE), 1)
    out = []
    for tile in range(groups // per):
        total = None
        for k in range(per):
            piece = acc[tile * per + k, :rows]
            shift = (k * width - start) % LANE
            if shift:
                piece = pltpu.roll(piece, shift, 1)
            total = piece if total is None else jnp.where(lane >= k * width, piece, total)
        out.append(total)
    return jnp.concatenate(out, axis=1)


def list_blocks(label, groups, start, order, column, head, follow):
    sources = label.shape[1]

    @pl.loop(0, groups)
    def _(r):
        start[r] = 0
        head[r] = -1

    def each(act):
        @pl.loop(0, sources)
        def _(source):
            for k in range(2):
                at = label[k, source]

                @pl.when(at >= 0)
                def _():
                    act(2 * source + k, at // groups, at % groups)

    def count(slot, r, c):
        start[r] += 1
        follow[slot] = head[c]
        head[c] = slot

    def place(slot, r, c):
        at = start[r] - 1
        start[r] = at
        order[at] = slot
        column[at] = c

    each(count)
    start[groups] = 0

    @pl.loop(0, groups)
    def _(r):
        start[groups] += start[r]
        start[r] = start[groups]

    each(place)


def panel_kernel(
    pivots, arrived, entries, inverse, factor, second, code, label, start, order, column, head, follow,
    acc, marks, load, later, result, sem,
):
    groups, rows, _ = entries.shape
    sources = arrived.shape[0]
    block_rows = rows // groups
    dead = 2 * pivots
    inverse_copy = pltpu.make_async_copy(inverse.at[0, 0], load, sem.at[1])
    inverse_copy.start()

    shape = (sources, LABELROWS, LANE)
    own = lax.broadcasted_iota(jnp.int32, shape, 0) == lax.broadcasted_iota(jnp.int32, shape, 2)
    sent = arrived[:, 2 * block_rows :, :].astype(jnp.float32)
    label[...] = jnp.sum(jnp.where(own, sent, 0.0), axis=0).astype(jnp.int32) - 1
    copy = pltpu.make_async_copy(label, marks, sem.at[0])
    copy.start()
    acc[:, :rows] = entries[...].astype(jnp.float32)
    copy.wait()

    @pl.loop(0, sources, unroll=4)
    def _(source):
        for k in range(2):
            at = marks[k, source]
            at = jnp.where(at < 0, groups * groups, at)
            r, c = at // groups, at % groups
            where = pl.ds(pl.multiple_of(r * block_rows, block_rows), block_rows)
            block = arrived[source, k * block_rows : (k + 1) * block_rows, :]
            acc[c, where, :] += block.astype(jnp.float32)

    later[...] = gather_lanes(acc, rows, pivots, pivots, groups)
    later_copy = pltpu.make_async_copy(later, second, sem.at[2])
    later_copy.start()
    columns = gather_lanes(acc, rows, 0, pivots, groups)
    inverse_copy.wait()
    result[...] = dot3(split(columns), split(load[...]))
    result_copy = pltpu.make_async_copy(result, factor, sem.at[3])
    result_copy.start()
    codes, exponents = encode(result[...])
    later_codes, later_exponents = encode(later[...])
    kept, kept_later = rows - pivots, rows - dead
    code[:kept] = codes[pivots:]
    code[kept : kept + kept_later] = later_codes[dead:]
    row = lax.broadcasted_iota(jnp.int32, exponents.shape, 0)
    code[kept + kept_later :] = jnp.where(row == 0, exponents, later_exponents).astype(jnp.int16)
    list_blocks(marks, groups, start, order, column, head, follow)
    later_copy.wait()
    result_copy.wait()


def left_kernel(pivots, gathered, factor, second, inverse, factors, left, pivot_code, exponent, sem):
    groups, code_rows, _ = gathered.shape
    rows, panel = factor.shape
    copies = [
        pltpu.make_async_copy(gathered.at[:, pl.ds(0, pivots), :], pivot_code, sem.at[0]),
        pltpu.make_async_copy(
            gathered.at[:, pl.ds(code_rows - ROWTILE, ROWTILE), :], exponent, sem.at[1]
        ),
    ]
    for copy in copies:
        copy.start()
    factors[0, 0] = factor[...]
    for copy in copies:
        copy.wait()
    lane = lax.broadcasted_iota(jnp.int32, (ROWTILE, panel), 1)
    total = jnp.zeros((ROWTILE, panel), jnp.float32)
    for g in range(groups):
        scale = pltpu.roll(scale_of(exponent[g]), (g * pivots - pivots) % panel, 1)
        total = jnp.where((lane >= g * pivots) & (lane < (g + 1) * pivots), scale, total)
    scale = total[:1]
    pivot_rows = split_code(pivot_code[...].reshape(groups * pivots, panel))
    inverse_parts = split(inverse[0, 0])
    first = factor[pivots:]
    update = dot3(split(first), pivot_rows) * scale
    result = dot3(split(second[pivots:] - update), inverse_parts)
    factors[0, 1, :pivots] = jnp.zeros((pivots, panel), jnp.float32)
    factors[0, 1, pivots:] = result
    own = dot3(split(result[pivots:]), inverse_parts, NN)
    mixed = first[pivots:] - dot3(split(own * scale), pivot_rows, NN)
    for k, part in enumerate((mixed, own)):
        high, low = split(part)
        left[k, :, :panel] = high
        left[k, :, panel : 2 * panel] = high
        left[k, :, 2 * panel :] = low


def update_kernel(
    pivots, label, head, follow, left, code, front, first, middle, base, edge, open_, right, acc
):
    rows, panel = right.shape[1], code.shape[2]
    groups = head.shape[0]
    block_rows = rows // groups
    dead = 2 * pivots
    step = pl.program_id(0)

    @pl.when(step == 0)
    def _():
        right[...] = jnp.zeros(right.shape, jnp.bfloat16)

    for d in range(2):
        acc[d] = front[0, :, d * rows : d * rows + 2 * LANE].astype(jnp.float32)

        def add(slot, d=d):
            k = slot % 2
            r = label[k, slot // 2] // groups
            where = pl.ds(pl.multiple_of(r * block_rows, block_rows), block_rows)
            source = pl.ds(pl.multiple_of(k * block_rows, block_rows), block_rows)
            acc[d, where, :LANE] += first[slot // 2, source, :].astype(jnp.float32)
            acc[d, where, LANE:] += middle[slot].astype(jnp.float32)
            return follow[slot]

        lax.while_loop(lambda slot: slot >= 0, add, head[2 * step + d])

    kept = (rows - pivots, rows - dead)
    starts = (0, kept[0])
    sides = []
    for d in range(2):
        scale = scale_of(code[d, kept[0] + kept[1] :])
        columns = slice(d * rows + 2 * LANE, (d + 1) * rows)
        total = jnp.concatenate(
            [acc[d, dead:], front[0, dead:, columns].astype(jnp.float32)], axis=1
        )
        for k in range(2):
            high, low = split_code(code[d, starts[k] : starts[k] + kept[k]])
            right[k, rows - kept[k] :, :panel] = high
            right[k, rows - kept[k] :, panel : 2 * panel] = low
            right[k, rows - kept[k] :, 2 * panel :] = high
            total = total - dot_nt(left[k], right[k]) * scale[k : k + 1]
        open_[d] = total[:, 2 * LANE :]
        sides.append(total.astype(jnp.bfloat16))
    even, odd = sides
    base[0] = jnp.concatenate([even[:, dead:], odd[:, dead:]], axis=1)
    edge[0] = jnp.concatenate([even[:, 2 * LANE - dead : 2 * LANE], odd[:, dead : 2 * dead]], axis=1)


def finish_kernel(pivots, start, order, column, rest, edge, open_, base, out, acc, even, odd, sem):
    groups, step_rows, width = acc.shape
    block_rows = rest.shape[1]
    dead = 2 * pivots
    pair_width = base.shape[2] // (groups // 2)
    per = step_rows // block_rows
    step, steps = pl.program_id(0), pl.num_programs(0)
    row = step * per + groups - steps * per
    acc[...] = jnp.zeros(acc.shape, jnp.float32)
    for p in range(per):

        @pl.loop(start[row + p], start[row + p + 1])
        def _(i):
            block = rest[order[i]].astype(jnp.float32)
            acc[column[i], p * block_rows : (p + 1) * block_rows, :] += block

    def copies(at, m):
        here = pl.ds(pl.multiple_of(at * step_rows, ROWTILE), step_rows)
        first = m * pair_width + LANE
        last = (m + 1) * pair_width - width
        return (
            pltpu.make_async_copy(
                even.at[at, m], out.at[0, here, pl.ds(first, even.shape[3])], sem.at[at, m]
            ),
            pltpu.make_async_copy(
                odd.at[at, m], out.at[0, here, pl.ds(last, width)], sem.at[at, groups // 2 + m]
            ),
        )

    for m in range(groups // 2):
        low = (open_[2 * m] + acc[2 * m]).astype(jnp.bfloat16)
        even[step, m] = jnp.concatenate([edge[m, :, :dead], low, edge[m, :, dead:]], axis=1)
        odd[step, m] = (open_[2 * m + 1] + acc[2 * m + 1]).astype(jnp.bfloat16)
        for copy in copies(step, m):
            copy.start()

    @pl.when(step == steps - 1)
    def _():
        @pl.loop(0, steps)
        def _(at):
            for m in range(groups // 2):
                for copy in copies(at, m):
                    copy.wait()


def local(front_entries, child_blocks, dest_device, dest_tile, child_count, diag_inverse):
    grp_total = lax.axis_size("grp")
    device_total = grp_total * lax.axis_size("front")
    axes = ("front", "grp")
    slots, block_rows, block_cols = child_blocks.shape
    _, rows, width = front_entries.shape
    panel = diag_inverse.shape[2]
    pivots = panel // grp_total
    slot_count = 2 * device_total
    rest_cols = block_cols - 2 * LANE
    hbm = pl.BlockSpec(memory_space=pl.ANY)
    smem = pl.BlockSpec(memory_space=pltpu.SMEM)
    whole = lambda *shape: pl.BlockSpec(shape, lambda i: (0,) * len(shape))

    first_rows = 2 * block_rows + LABELROWS
    first_out, position = pl.pallas_call(
        pack_first_kernel,
        grid=(1,),
        out_shape=(
            jax.ShapeDtypeStruct((device_total, first_rows, LANE), jnp.bfloat16),
            jax.ShapeDtypeStruct((slots,), jnp.int32),
        ),
        in_specs=[smem, smem, smem, hbm],
        out_specs=(whole(device_total, first_rows, LANE), smem),
        scratch_shapes=[
            pltpu.VMEM((slots, block_rows, LANE), jnp.bfloat16),
            pltpu.SMEM((3, device_total), jnp.int32),
            pltpu.SemaphoreType.DMA,
        ],
        compiler_params=params(),
        name="pack_first",
    )(child_count, dest_device.reshape(slots), dest_tile, child_blocks)
    first = lax.all_to_all(first_out, axes, split_axis=0, concat_axis=0, tiled=True)
    middle_out, rest_out, entries = pl.pallas_call(
        pack_rest_kernel,
        grid=(1,),
        out_shape=(
            jax.ShapeDtypeStruct((slot_count, block_rows, LANE), jnp.bfloat16),
            jax.ShapeDtypeStruct((slot_count, block_rows, rest_cols), jnp.bfloat16),
            jax.ShapeDtypeStruct((grp_total, rows, LANE), jnp.bfloat16),
        ),
        in_specs=[smem, whole(*child_blocks.shape), hbm],
        out_specs=(
            whole(slot_count, block_rows, LANE),
            whole(slot_count, block_rows, rest_cols),
            whole(grp_total, rows, LANE),
        ),
        scratch_shapes=[pltpu.SemaphoreType.DMA((grp_total,))],
        compiler_params=params(),
        cost_estimate=pl.CostEstimate(flops=0, bytes_accessed=16 * 2**20, transcendentals=0),
        name="pack_rest",
    )(position, child_blocks, front_entries)
    middle = lax.all_to_all(middle_out, axes, split_axis=0, concat_axis=0, tiled=True)
    first, rest_out, entries = lax.optimization_barrier((first, rest_out, entries))

    kept = rows - 2 * pivots
    code_rows = (rows - pivots) + kept + ROWTILE
    inverse_spec = lambda k: pl.BlockSpec((1, 1, panel, panel), lambda i: (0, k, 0, 0))
    row_blocks = rows // block_rows
    lengths = (row_blocks + 1, slot_count, slot_count, row_blocks, slot_count)
    factor, second, code, label, start, order, column, head, follow = pl.pallas_call(
        functools.partial(panel_kernel, pivots),
        grid=(1,),
        out_shape=(
            jax.ShapeDtypeStruct((rows, panel), jnp.float32),
            jax.ShapeDtypeStruct((rows, panel), jnp.float32),
            jax.ShapeDtypeStruct((code_rows, panel), jnp.int16),
            jax.ShapeDtypeStruct((LABELROWS, LANE), jnp.int32),
            *(jax.ShapeDtypeStruct((length,), jnp.int32) for length in lengths),
        ),
        in_specs=[whole(*first.shape), whole(*entries.shape), hbm],
        out_specs=(hbm, hbm, whole(code_rows, panel), whole(LABELROWS, LANE)) + (smem,) * 5,
        scratch_shapes=[
            pltpu.VMEM((grp_total, rows + block_rows, LANE), jnp.float32),
            pltpu.SMEM((LABELROWS, LANE), jnp.int32),
            pltpu.VMEM((panel, panel), jnp.float32),
            pltpu.VMEM((rows, panel), jnp.float32),
            pltpu.VMEM((rows, panel), jnp.float32),
            pltpu.SemaphoreType.DMA((4,)),
        ],
        compiler_params=params(),
        cost_estimate=pl.CostEstimate(flops=2 * 10**9, bytes_accessed=10 * 2**20, transcendentals=0),
        name="panels",
    )(first, entries, diag_inverse)
    gathered = lax.all_gather(code, "grp", axis=0, tiled=False)

    gathered, rest_out = lax.optimization_barrier((gathered, rest_out))
    rest = lax.all_to_all(rest_out, axes, split_axis=0, concat_axis=0, tiled=True)

    factors, left = pl.pallas_call(
        functools.partial(left_kernel, pivots),
        grid=(1,),
        out_shape=(
            jax.ShapeDtypeStruct((1, 2, rows, panel), jnp.float32),
            jax.ShapeDtypeStruct((2, kept, 3 * panel), jnp.bfloat16),
        ),
        in_specs=[hbm, whole(rows, panel), whole(rows, panel), inverse_spec(1)],
        out_specs=(whole(1, 2, rows, panel), whole(2, kept, 3 * panel)),
        scratch_shapes=[
            pltpu.VMEM((grp_total, pivots, panel), jnp.int16),
            pltpu.VMEM((grp_total, ROWTILE, panel), jnp.int16),
            pltpu.SemaphoreType.DMA((2,)),
        ],
        compiler_params=params(),
        cost_estimate=pl.CostEstimate(flops=4 * 10**9, bytes_accessed=8 * 2**20, transcendentals=0),
        name="left_factors",
    )(gathered, factor, second, diag_inverse)

    base, edge, open_ = pl.pallas_call(
        functools.partial(update_kernel, pivots),
        grid=(grp_total // 2,),
        out_shape=(
            jax.ShapeDtypeStruct((1, kept, grp_total * kept), jnp.bfloat16),
            jax.ShapeDtypeStruct((grp_total // 2, kept, LANE), jnp.bfloat16),
            jax.ShapeDtypeStruct((grp_total, kept, rest_cols), jnp.float32),
        ),
        in_specs=[
            smem,
            smem,
            smem,
            whole(2, kept, 3 * panel),
            pl.BlockSpec((2, code_rows, panel), lambda i: (i, 0, 0)),
            pl.BlockSpec((1, rows, 2 * rows), lambda i: (0, 0, i)),
            whole(*first.shape),
            whole(*middle.shape),
        ],
        out_specs=(
            pl.BlockSpec((1, kept, 2 * kept), lambda i: (0, 0, i)),
            pl.BlockSpec((1, kept, LANE), lambda i: (i, 0, 0)),
            pl.BlockSpec((2, kept, rest_cols), lambda i: (i, 0, 0)),
        ),
        scratch_shapes=[
            pltpu.VMEM((2, rows, 3 * panel), jnp.bfloat16),
            pltpu.VMEM((2, rows, 2 * LANE), jnp.float32),
        ],
        compiler_params=params(),
        cost_estimate=pl.CostEstimate(flops=20 * 10**9, bytes_accessed=40 * 2**20, transcendentals=0),
        name="update",
    )(label, head, follow, left, gathered, front_entries, first, middle)

    step_rows = kept // 2
    schur = pl.pallas_call(
        functools.partial(finish_kernel, pivots),
        grid=(kept // step_rows,),
        out_shape=jax.ShapeDtypeStruct((1, kept, grp_total * kept), jnp.bfloat16),
        in_specs=[
            smem,
            smem,
            smem,
            whole(*rest.shape),
            pl.BlockSpec((grp_total // 2, step_rows, LANE), lambda i: (0, i, 0)),
            pl.BlockSpec((grp_total, step_rows, rest_cols), lambda i: (0, i, 0)),
            hbm,
        ],
        out_specs=hbm,
        input_output_aliases={6: 0},
        scratch_shapes=[
            pltpu.VMEM((grp_total, step_rows, rest_cols), jnp.float32),
            pltpu.VMEM((2, grp_total // 2, step_rows, rest_cols + LANE), jnp.bfloat16),
            pltpu.VMEM((2, grp_total // 2, step_rows, rest_cols), jnp.bfloat16),
            pltpu.SemaphoreType.DMA((2, grp_total)),
        ],
        compiler_params=params(),
        cost_estimate=pl.CostEstimate(flops=10**7, bytes_accessed=30 * 2**20, transcendentals=0),
        name="finish",
    )(start, order, column, rest, edge, open_, base)
    return schur, factors


def solution(mesh):
    placed = (
        P("front", "grp", None),
        P(("front", "grp"), None, None),
        P(("front", "grp"), None),
        P(("front", "grp")),
        P(("front", "grp")),
        P("front", None, None, None),
    )
    return jax.shard_map(
        local,
        mesh=mesh,
        in_specs=placed,
        out_specs=(P("front", "grp", None), P("front", None, "grp", None)),
        check_vma=False,
    )
```

```python
import functools

import jax
import jax.numpy as jnp
from jax import lax
from jax.experimental import pallas as pl
from jax.experimental.pallas import tpu as pltpu
from jax.sharding import PartitionSpec as P

LANE = 128
ROWTILE = 16
LABELROWS = ROWTILE
MIB = 1024 * 1024
NT = (((1,), (1,)), ((), ()))
NN = (((1,), (0,)), ((), ()))


def params(mebibytes=56):
    return pltpu.CompilerParams(vmem_limit_bytes=mebibytes * MIB)


def split(x):
    high = x.astype(jnp.bfloat16)
    return high, (x - high.astype(jnp.float32)).astype(jnp.bfloat16)


def dot_nt(a, b, form=NT):
    return lax.dot_general(a, b, form, preferred_element_type=jnp.float32)


def dot3(a, b, form=NT):
    a_high, a_low = a
    b_high, b_low = b
    return dot_nt(a_high, b_high, form) + (
        dot_nt(a_high, b_low, form) + dot_nt(a_low, b_high, form)
    )


def split_code(code):
    return split(code.astype(jnp.int32).astype(jnp.float32))


def encode(x):
    rows = x.shape[0]
    largest = jnp.max(jnp.abs(x), axis=1, keepdims=True)
    exponent = jnp.ceil(jnp.log2(jnp.clip(largest, 1e-30, 1e38)))
    scaled = jnp.round(x * jnp.exp2(15.0 - exponent))
    code = jnp.clip(scaled, -32767.0, 32767.0).astype(jnp.int32).astype(jnp.int16)
    along = jnp.transpose(jnp.broadcast_to(exponent, (rows, LANE)))[:ROWTILE]
    return code, along.astype(jnp.int32)


def scale_of(exponent):
    return jnp.exp2(exponent.astype(jnp.int32).astype(jnp.float32) - 15.0)


def pack_first_kernel(count, target, tile, blocks, out, position, load, marks, sem):
    devices = out.shape[0]
    slots, rows, _ = blocks.shape
    copy = pltpu.make_async_copy(blocks.at[:, :, pl.ds(0, LANE)], load, sem)
    copy.start()

    @pl.loop(0, devices, unroll=8)
    def _(t):
        marks[2, t] = 2 * t
        marks[0, t] = 0
        marks[1, t] = 0

    @pl.loop(0, slots, unroll=4)
    def _(i):
        t = target[i]
        at = marks[2, t]
        marks[2, t] = at + 1
        position[i] = at
        marks[at % 2, t] = jnp.where(i < count[0], tile[i] + 1, 0)

    row = lax.broadcasted_iota(jnp.int32, (LABELROWS, LANE), 0)

    @pl.loop(0, devices, unroll=8)
    def _(t):
        both = jnp.where(row == 0, marks[0, t], jnp.where(row == 1, marks[1, t], 0))
        out[t, 2 * rows :, :] = both.astype(jnp.float32).astype(jnp.bfloat16)

    copy.wait()

    @pl.loop(0, slots, unroll=4)
    def _(i):
        at = position[i]
        out[at // 2, pl.ds(pl.multiple_of((at % 2) * rows, rows), rows), :] = load[i]


def pack_rest_kernel(position, blocks, front, middle, rest, entries, sem):
    groups = entries.shape[0]
    width = front.shape[2] // groups

    def copy(c):
        return pltpu.make_async_copy(
            front.at[0, :, pl.ds(c * width, LANE)], entries.at[c], sem.at[c]
        )

    for c in range(groups):
        copy(c).start()

    @pl.loop(0, blocks.shape[0], unroll=2)
    def _(i):
        at = position[i]
        middle[at] = blocks[i, :, LANE : 2 * LANE]
        rest[at] = blocks[i, :, 2 * LANE :]

    for c in range(groups):
        copy(c).wait()


def gather_lanes(acc, rows, start, width, groups):
    per = LANE // width
    lane = lax.broadcasted_iota(jnp.int32, (rows, LANE), 1)
    out = []
    for tile in range(groups // per):
        total = None
        for k in range(per):
            piece = acc[tile * per + k, :rows]
            shift = (k * width - start) % LANE
            if shift:
                piece = pltpu.roll(piece, shift, 1)
            total = piece if total is None else jnp.where(lane >= k * width, piece, total)
        out.append(total)
    return jnp.concatenate(out, axis=1)


def list_blocks(label, groups, start, order, column, head, follow):
    sources = label.shape[1]

    @pl.loop(0, groups)
    def _(r):
        start[r] = 0
        head[r] = -1

    def each(act):
        @pl.loop(0, sources)
        def _(source):
            for k in range(2):
                at = label[k, source]

                @pl.when(at >= 0)
                def _():
                    act(2 * source + k, at // groups, at % groups)

    def count(slot, r, c):
        start[r] += 1
        follow[slot] = head[c]
        head[c] = slot

    def place(slot, r, c):
        at = start[r] - 1
        start[r] = at
        order[at] = slot
        column[at] = c

    each(count)
    start[groups] = 0

    @pl.loop(0, groups)
    def _(r):
        start[groups] += start[r]
        start[r] = start[groups]

    each(place)


def panel_kernel(
    pivots, arrived, entries, inverse, factor, second, code, label, start, order, column, head, follow,
    acc, marks, load, later, result, sem,
):
    groups, rows, _ = entries.shape
    sources = arrived.shape[0]
    block_rows = rows // groups
    dead = 2 * pivots
    inverse_copy = pltpu.make_async_copy(inverse.at[0, 0], load, sem.at[1])
    inverse_copy.start()

    shape = (sources, LABELROWS, LANE)
    own = lax.broadcasted_iota(jnp.int32, shape, 0) == lax.broadcasted_iota(jnp.int32, shape, 2)
    sent = arrived[:, 2 * block_rows :, :].astype(jnp.float32)
    label[...] = jnp.sum(jnp.where(own, sent, 0.0), axis=0).astype(jnp.int32) - 1
    copy = pltpu.make_async_copy(label, marks, sem.at[0])
    copy.start()
    acc[:, :rows] = entries[...].astype(jnp.float32)
    copy.wait()

    @pl.loop(0, sources, unroll=4)
    def _(source):
        for k in range(2):
            at = marks[k, source]
            at = jnp.where(at < 0, groups * groups, at)
            r, c = at // groups, at % groups
            where = pl.ds(pl.multiple_of(r * block_rows, block_rows), block_rows)
            block = arrived[source, k * block_rows : (k + 1) * block_rows, :]
            acc[c, where, :] += block.astype(jnp.float32)

    later[...] = gather_lanes(acc, rows, pivots, pivots, groups)
    later_copy = pltpu.make_async_copy(later, second, sem.at[2])
    later_copy.start()
    columns = gather_lanes(acc, rows, 0, pivots, groups)
    inverse_copy.wait()
    result[...] = dot3(split(columns), split(load[...]))
    result_copy = pltpu.make_async_copy(result, factor, sem.at[3])
    result_copy.start()
    codes, exponents = encode(result[...])
    later_codes, later_exponents = encode(later[...])
    kept, kept_later = rows - pivots, rows - dead
    code[:kept] = codes[pivots:]
    code[kept : kept + kept_later] = later_codes[dead:]
    row = lax.broadcasted_iota(jnp.int32, exponents.shape, 0)
    code[kept + kept_later :] = jnp.where(row == 0, exponents, later_exponents).astype(jnp.int16)
    list_blocks(marks, groups, start, order, column, head, follow)
    later_copy.wait()
    result_copy.wait()


def left_kernel(pivots, gathered, factor, second, inverse, factors, left, pivot_code, exponent, sem):
    groups, code_rows, _ = gathered.shape
    rows, panel = factor.shape
    copies = [
        pltpu.make_async_copy(gathered.at[:, pl.ds(0, pivots), :], pivot_code, sem.at[0]),
        pltpu.make_async_copy(
            gathered.at[:, pl.ds(code_rows - ROWTILE, ROWTILE), :], exponent, sem.at[1]
        ),
    ]
    for copy in copies:
        copy.start()
    factors[0, 0] = factor[...]
    for copy in copies:
        copy.wait()
    lane = lax.broadcasted_iota(jnp.int32, (ROWTILE, panel), 1)
    total = jnp.zeros((ROWTILE, panel), jnp.float32)
    for g in range(groups):
        scale = pltpu.roll(scale_of(exponent[g]), (g * pivots - pivots) % panel, 1)
        total = jnp.where((lane >= g * pivots) & (lane < (g + 1) * pivots), scale, total)
    scale = total[:1]
    pivot_rows = split_code(pivot_code[...].reshape(groups * pivots, panel))
    inverse_parts = split(inverse[0, 0])
    first = factor[pivots:]
    update = dot3(split(first), pivot_rows) * scale
    result = dot3(split(second[pivots:] - update), inverse_parts)
    factors[0, 1, :pivots] = jnp.zeros((pivots, panel), jnp.float32)
    factors[0, 1, pivots:] = result
    own = dot3(split(result[pivots:]), inverse_parts, NN)
    mixed = first[pivots:] - dot3(split(own * scale), pivot_rows, NN)
    for k, part in enumerate((mixed, own)):
        high, low = split(part)
        left[k, :, :panel] = high
        left[k, :, panel : 2 * panel] = high
        left[k, :, 2 * panel :] = low


def update_kernel(
    pivots, label, head, follow, left, code, front, first, middle, base, edge, open_, right, acc
):
    rows, panel = right.shape[1], code.shape[2]
    groups = head.shape[0]
    block_rows = rows // groups
    dead = 2 * pivots
    step = pl.program_id(0)

    @pl.when(step == 0)
    def _():
        right[...] = jnp.zeros(right.shape, jnp.bfloat16)

    for d in range(2):
        acc[d] = front[0, :, d * rows : d * rows + 2 * LANE].astype(jnp.float32)

        def add(slot, d=d):
            k = slot % 2
            r = label[k, slot // 2] // groups
            where = pl.ds(pl.multiple_of(r * block_rows, block_rows), block_rows)
            source = pl.ds(pl.multiple_of(k * block_rows, block_rows), block_rows)
            acc[d, where, :LANE] += first[slot // 2, source, :].astype(jnp.float32)
            acc[d, where, LANE:] += middle[slot].astype(jnp.float32)
            return follow[slot]

        lax.while_loop(lambda slot: slot >= 0, add, head[2 * step + d])

    kept = (rows - pivots, rows - dead)
    starts = (0, kept[0])
    sides = []
    for d in range(2):
        scale = scale_of(code[d, kept[0] + kept[1] :])
        columns = slice(d * rows + 2 * LANE, (d + 1) * rows)
        total = jnp.concatenate(
            [acc[d, dead:], front[0, dead:, columns].astype(jnp.float32)], axis=1
        )
        for k in range(2):
            high, low = split_code(code[d, starts[k] : starts[k] + kept[k]])
            right[k, rows - kept[k] :, :panel] = high
            right[k, rows - kept[k] :, panel : 2 * panel] = low
            right[k, rows - kept[k] :, 2 * panel :] = high
            total = total - dot_nt(left[k], right[k]) * scale[k : k + 1]
        open_[d] = total[:, 2 * LANE :]
        sides.append(total.astype(jnp.bfloat16))
    even, odd = sides
    base[0] = jnp.concatenate([even[:, dead:], odd[:, dead:]], axis=1)
    edge[0] = jnp.concatenate([even[:, 2 * LANE - dead : 2 * LANE], odd[:, dead : 2 * dead]], axis=1)


def finish_kernel(pivots, start, order, column, rest, edge, open_, base, out, acc, even, odd, sem):
    groups, step_rows, width = acc.shape
    block_rows = rest.shape[1]
    dead = 2 * pivots
    pair_width = base.shape[2] // (groups // 2)
    per = step_rows // block_rows
    step, steps = pl.program_id(0), pl.num_programs(0)
    row = step * per + groups - steps * per
    acc[...] = jnp.zeros(acc.shape, jnp.float32)
    for p in range(per):

        @pl.loop(start[row + p], start[row + p + 1])
        def _(i):
            block = rest[order[i]].astype(jnp.float32)
            acc[column[i], p * block_rows : (p + 1) * block_rows, :] += block

    def copies(at, m):
        here = pl.ds(pl.multiple_of(at * step_rows, ROWTILE), step_rows)
        first = m * pair_width + LANE
        last = (m + 1) * pair_width - width
        return (
            pltpu.make_async_copy(
                even.at[at, m], out.at[0, here, pl.ds(first, even.shape[3])], sem.at[at, m]
            ),
            pltpu.make_async_copy(
                odd.at[at, m], out.at[0, here, pl.ds(last, width)], sem.at[at, groups // 2 + m]
            ),
        )

    for m in range(groups // 2):
        low = (open_[2 * m] + acc[2 * m]).astype(jnp.bfloat16)
        even[step, m] = jnp.concatenate([edge[m, :, :dead], low, edge[m, :, dead:]], axis=1)
        odd[step, m] = (open_[2 * m + 1] + acc[2 * m + 1]).astype(jnp.bfloat16)
        for copy in copies(step, m):
            copy.start()

    @pl.when(step == steps - 1)
    def _():
        @pl.loop(0, steps)
        def _(at):
            for m in range(groups // 2):
                for copy in copies(at, m):
                    copy.wait()


def local(front_entries, child_blocks, dest_device, dest_tile, child_count, diag_inverse):
    grp_total = lax.axis_size("grp")
    device_total = grp_total * lax.axis_size("front")
    axes = ("front", "grp")
    slots, block_rows, block_cols = child_blocks.shape
    _, rows, width = front_entries.shape
    panel = diag_inverse.shape[2]
    pivots = panel // grp_total
    slot_count = 2 * device_total
    rest_cols = block_cols - 2 * LANE
    hbm = pl.BlockSpec(memory_space=pl.ANY)
    smem = pl.BlockSpec(memory_space=pltpu.SMEM)
    whole = lambda *shape: pl.BlockSpec(shape, lambda i: (0,) * len(shape))

    first_rows = 2 * block_rows + LABELROWS
    first_out, position = pl.pallas_call(
        pack_first_kernel,
        grid=(1,),
        out_shape=(
            jax.ShapeDtypeStruct((device_total, first_rows, LANE), jnp.bfloat16),
            jax.ShapeDtypeStruct((slots,), jnp.int32),
        ),
        in_specs=[smem, smem, smem, hbm],
        out_specs=(whole(device_total, first_rows, LANE), smem),
        scratch_shapes=[
            pltpu.VMEM((slots, block_rows, LANE), jnp.bfloat16),
            pltpu.SMEM((3, device_total), jnp.int32),
            pltpu.SemaphoreType.DMA,
        ],
        compiler_params=params(),
        name="pack_first",
    )(child_count, dest_device.reshape(slots), dest_tile, child_blocks)
    first = lax.all_to_all(first_out, axes, split_axis=0, concat_axis=0, tiled=True)
    middle_out, rest_out, entries = pl.pallas_call(
        pack_rest_kernel,
        grid=(1,),
        out_shape=(
            jax.ShapeDtypeStruct((slot_count, block_rows, LANE), jnp.bfloat16),
            jax.ShapeDtypeStruct((slot_count, block_rows, rest_cols), jnp.bfloat16),
            jax.ShapeDtypeStruct((grp_total, rows, LANE), jnp.bfloat16),
        ),
        in_specs=[smem, whole(*child_blocks.shape), hbm],
        out_specs=(
            whole(slot_count, block_rows, LANE),
            whole(slot_count, block_rows, rest_cols),
            whole(grp_total, rows, LANE),
        ),
        scratch_shapes=[pltpu.SemaphoreType.DMA((grp_total,))],
        compiler_params=params(),
        cost_estimate=pl.CostEstimate(flops=0, bytes_accessed=16 * 2**20, transcendentals=0),
        name="pack_rest",
    )(position, child_blocks, front_entries)
    middle = lax.all_to_all(middle_out, axes, split_axis=0, concat_axis=0, tiled=True)
    first, rest_out, entries = lax.optimization_barrier((first, rest_out, entries))

    kept = rows - 2 * pivots
    code_rows = (rows - pivots) + kept + ROWTILE
    inverse_spec = lambda k: pl.BlockSpec((1, 1, panel, panel), lambda i: (0, k, 0, 0))
    row_blocks = rows // block_rows
    lengths = (row_blocks + 1, slot_count, slot_count, row_blocks, slot_count)
    factor, second, code, label, start, order, column, head, follow = pl.pallas_call(
        functools.partial(panel_kernel, pivots),
        grid=(1,),
        out_shape=(
            jax.ShapeDtypeStruct((rows, panel), jnp.float32),
            jax.ShapeDtypeStruct((rows, panel), jnp.float32),
            jax.ShapeDtypeStruct((code_rows, panel), jnp.int16),
            jax.ShapeDtypeStruct((LABELROWS, LANE), jnp.int32),
            *(jax.ShapeDtypeStruct((length,), jnp.int32) for length in lengths),
        ),
        in_specs=[whole(*first.shape), whole(*entries.shape), hbm],
        out_specs=(hbm, hbm, whole(code_rows, panel), whole(LABELROWS, LANE)) + (smem,) * 5,
        scratch_shapes=[
            pltpu.VMEM((grp_total, rows + block_rows, LANE), jnp.float32),
            pltpu.SMEM((LABELROWS, LANE), jnp.int32),
            pltpu.VMEM((panel, panel), jnp.float32),
            pltpu.VMEM((rows, panel), jnp.float32),
            pltpu.VMEM((rows, panel), jnp.float32),
            pltpu.SemaphoreType.DMA((4,)),
        ],
        compiler_params=params(),
        cost_estimate=pl.CostEstimate(flops=2 * 10**9, bytes_accessed=10 * 2**20, transcendentals=0),
        name="panels",
    )(first, entries, diag_inverse)
    gathered = lax.all_gather(code, "grp", axis=0, tiled=False)

    gathered, rest_out = lax.optimization_barrier((gathered, rest_out))
    rest = lax.all_to_all(rest_out, axes, split_axis=0, concat_axis=0, tiled=True)

    factors, left = pl.pallas_call(
        functools.partial(left_kernel, pivots),
        grid=(1,),
        out_shape=(
            jax.ShapeDtypeStruct((1, 2, rows, panel), jnp.float32),
            jax.ShapeDtypeStruct((2, kept, 3 * panel), jnp.bfloat16),
        ),
        in_specs=[hbm, whole(rows, panel), whole(rows, panel), inverse_spec(1)],
        out_specs=(whole(1, 2, rows, panel), whole(2, kept, 3 * panel)),
        scratch_shapes=[
            pltpu.VMEM((grp_total, pivots, panel), jnp.int16),
            pltpu.VMEM((grp_total, ROWTILE, panel), jnp.int16),
            pltpu.SemaphoreType.DMA((2,)),
        ],
        compiler_params=params(),
        cost_estimate=pl.CostEstimate(flops=4 * 10**9, bytes_accessed=8 * 2**20, transcendentals=0),
        name="left_factors",
    )(gathered, factor, second, diag_inverse)

    base, edge, open_ = pl.pallas_call(
        functools.partial(update_kernel, pivots),
        grid=(grp_total // 2,),
        out_shape=(
            jax.ShapeDtypeStruct((1, kept, grp_total * kept), jnp.bfloat16),
            jax.ShapeDtypeStruct((grp_total // 2, kept, LANE), jnp.bfloat16),
            jax.ShapeDtypeStruct((grp_total, kept, rest_cols), jnp.float32),
        ),
        in_specs=[
            smem,
            smem,
            smem,
            whole(2, kept, 3 * panel),
            pl.BlockSpec((2, code_rows, panel), lambda i: (i, 0, 0)),
            pl.BlockSpec((1, rows, 2 * rows), lambda i: (0, 0, i)),
            whole(*first.shape),
            whole(*middle.shape),
        ],
        out_specs=(
            pl.BlockSpec((1, kept, 2 * kept), lambda i: (0, 0, i)),
            pl.BlockSpec((1, kept, LANE), lambda i: (i, 0, 0)),
            pl.BlockSpec((2, kept, rest_cols), lambda i: (i, 0, 0)),
        ),
        scratch_shapes=[
            pltpu.VMEM((2, rows, 3 * panel), jnp.bfloat16),
            pltpu.VMEM((2, rows, 2 * LANE), jnp.float32),
        ],
        compiler_params=params(),
        cost_estimate=pl.CostEstimate(flops=20 * 10**9, bytes_accessed=40 * 2**20, transcendentals=0),
        name="update",
    )(label, head, follow, left, gathered, front_entries, first, middle)

    step_rows = kept // 2
    schur = pl.pallas_call(
        functools.partial(finish_kernel, pivots),
        grid=(kept // step_rows,),
        out_shape=jax.ShapeDtypeStruct((1, kept, grp_total * kept), jnp.bfloat16),
        in_specs=[
            smem,
            smem,
            smem,
            whole(*rest.shape),
            pl.BlockSpec((grp_total // 2, step_rows, LANE), lambda i: (0, i, 0)),
            pl.BlockSpec((grp_total, step_rows, rest_cols), lambda i: (0, i, 0)),
            hbm,
        ],
        out_specs=hbm,
        input_output_aliases={6: 0},
        scratch_shapes=[
            pltpu.VMEM((grp_total, step_rows, rest_cols), jnp.float32),
            pltpu.VMEM((2, grp_total // 2, step_rows, rest_cols + LANE), jnp.bfloat16),
            pltpu.VMEM((2, grp_total // 2, step_rows, rest_cols), jnp.bfloat16),
            pltpu.SemaphoreType.DMA((2, grp_total)),
        ],
        compiler_params=params(),
        cost_estimate=pl.CostEstimate(flops=10**7, bytes_accessed=30 * 2**20, transcendentals=0),
        name="finish",
    )(start, order, column, rest, edge, open_, base)
    return schur, factors


def solution(mesh):
    placed = (
        P("front", "grp", None),
        P(("front", "grp"), None, None),
        P(("front", "grp"), None),
        P(("front", "grp")),
        P(("front", "grp")),
        P("front", None, None, None),
    )
    return jax.shard_map(
        local,
        mesh=mesh,
        in_specs=placed,
        out_specs=(P("front", "grp", None), P("front", None, "grp", None)),
        check_vma=False,
    )
```

```python
import functools

import jax
import jax.numpy as jnp
from jax import lax
from jax.experimental import pallas as pl
from jax.experimental.pallas import tpu as pltpu
from jax.sharding import PartitionSpec as P

LANE = 128
ROWTILE = 16
LABELROWS = 8
MIB = 1024 * 1024
NT = (((1,), (1,)), ((), ()))
NN = (((1,), (0,)), ((), ()))


def params(mebibytes=56):
    return pltpu.CompilerParams(vmem_limit_bytes=mebibytes * MIB)


def split(x):
    high = x.astype(jnp.bfloat16)
    return high, (x - high.astype(jnp.float32)).astype(jnp.bfloat16)


def dot_nt(a, b, form=NT):
    return lax.dot_general(a, b, form, preferred_element_type=jnp.float32)


def dot3(a, b, form=NT):
    a_high, a_low = a
    b_high, b_low = b
    return dot_nt(a_high, b_high, form) + (
        dot_nt(a_high, b_low, form) + dot_nt(a_low, b_high, form)
    )


def split_code(code):
    return split(code.astype(jnp.int32).astype(jnp.float32))


def encode(x):
    rows = x.shape[0]
    largest = jnp.max(jnp.abs(x), axis=1, keepdims=True)
    exponent = jnp.ceil(jnp.log2(jnp.clip(largest, 1e-30, 1e38)))
    scaled = jnp.round(x * jnp.exp2(15.0 - exponent))
    code = jnp.clip(scaled, -32767.0, 32767.0).astype(jnp.int32).astype(jnp.int16)
    along = jnp.transpose(jnp.broadcast_to(exponent, (rows, LANE)))[:ROWTILE]
    return code, along.astype(jnp.int32)


def scale_of(exponent):
    return jnp.exp2(exponent.astype(jnp.int32).astype(jnp.float32) - 15.0)


def pack_first_kernel(count, target, tile, blocks, packed, position, load, out, marks, sem):
    devices = packed.shape[0]
    slots, rows, _ = blocks.shape
    copy = pltpu.make_async_copy(blocks.at[:, :, pl.ds(0, LANE)], load, sem)
    copy.start()

    @pl.loop(0, devices, unroll=8)
    def _(t):
        marks[2, t] = 2 * t
        marks[0, t] = 0
        marks[1, t] = 0

    @pl.loop(0, slots, unroll=4)
    def _(i):
        t = target[i]
        at = marks[2, t]
        marks[2, t] = at + 1
        position[i] = at
        marks[at % 2, t] = jnp.where(i < count[0], tile[i] + 1, 0)

    row = lax.broadcasted_iota(jnp.int32, (LABELROWS, LANE), 0)

    @pl.loop(0, devices, unroll=8)
    def _(t):
        both = jnp.where(row == 0, marks[0, t], jnp.where(row == 1, marks[1, t], 0))
        out[t, 2 * rows :, :] = both.astype(jnp.float32).astype(jnp.bfloat16)

    copy.wait()

    @pl.loop(0, slots, unroll=4)
    def _(i):
        at = position[i]
        out[at // 2, pl.ds(pl.multiple_of((at % 2) * rows, rows), rows), :] = load[i]

    copy = pltpu.make_async_copy(out.at[pl.ds(0, devices)], packed, sem)
    copy.start()
    copy.wait()


def pack_rest_kernel(position, blocks, front, middle, rest, entries, sem):
    groups = entries.shape[0]
    width = front.shape[2] // groups

    def copy(c):
        return pltpu.make_async_copy(
            front.at[0, :, pl.ds(c * width, LANE)], entries.at[c], sem.at[c]
        )

    for c in range(groups):
        copy(c).start()

    @pl.loop(0, blocks.shape[0], unroll=2)
    def _(i):
        at = position[i]
        middle[at] = blocks[i, :, LANE : 2 * LANE]
        rest[at] = blocks[i, :, 2 * LANE :]

    for c in range(groups):
        copy(c).wait()


def gather_lanes(acc, rows, start, width, groups):
    per = LANE // width
    lane = lax.broadcasted_iota(jnp.int32, (rows, LANE), 1)
    out = []
    for tile in range(groups // per):
        total = None
        for k in range(per):
            piece = acc[tile * per + k, :rows]
            shift = (k * width - start) % LANE
            if shift:
                piece = pltpu.roll(piece, shift, 1)
            total = piece if total is None else jnp.where(lane >= k * width, piece, total)
        out.append(total)
    return jnp.concatenate(out, axis=1)


def list_blocks(label, groups, start, order, column, head, follow):
    sources = label.shape[1]

    @pl.loop(0, groups)
    def _(r):
        start[r] = 0
        head[r] = -1

    def each(act):
        @pl.loop(0, sources)
        def _(source):
            for k in range(2):
                at = label[k, source]

                @pl.when(at >= 0)
                def _():
                    act(2 * source + k, at // groups, at % groups)

    def count(slot, r, c):
        start[r] += 1
        follow[slot] = head[c]
        head[c] = slot

    def place(slot, r, c):
        at = start[r] - 1
        start[r] = at
        order[at] = slot
        column[at] = c

    each(count)
    start[groups] = 0

    @pl.loop(0, groups)
    def _(r):
        start[groups] += start[r]
        start[r] = start[groups]

    each(place)


def panel_kernel(
    pivots, sent, entries, inverse, factor, second, code, label, start, order, column, head, follow,
    arrived, acc, marks, load, later, result, sem,
):
    groups, rows, _ = entries.shape
    sources = sent.shape[0]
    block_rows = rows // groups
    dead = 2 * pivots
    sent_copy = pltpu.make_async_copy(sent, arrived.at[pl.ds(0, sources)], sem.at[4])
    sent_copy.start()
    inverse_copy = pltpu.make_async_copy(inverse.at[0, 0], load, sem.at[1])
    inverse_copy.start()
    acc[:, :rows] = entries[...].astype(jnp.float32)
    sent_copy.wait()

    shape = (sources, LABELROWS, LANE)
    own = lax.broadcasted_iota(jnp.int32, shape, 0) == lax.broadcasted_iota(jnp.int32, shape, 2)
    marked = arrived[:sources, 2 * block_rows :, :].astype(jnp.float32)
    label[...] = jnp.sum(jnp.where(own, marked, 0.0), axis=0).astype(jnp.int32) - 1
    copy = pltpu.make_async_copy(label, marks, sem.at[0])
    copy.start()
    copy.wait()

    @pl.loop(0, sources, unroll=4)
    def _(source):
        for k in range(2):
            at = marks[k, source]
            at = jnp.where(at < 0, groups * groups, at)
            r, c = at // groups, at % groups
            where = pl.ds(pl.multiple_of(r * block_rows, block_rows), block_rows)
            block = arrived[source, k * block_rows : (k + 1) * block_rows, :]
            acc[c, where, :] += block.astype(jnp.float32)

    later[...] = gather_lanes(acc, rows, pivots, pivots, groups)
    later_copy = pltpu.make_async_copy(later, second, sem.at[2])
    later_copy.start()
    columns = gather_lanes(acc, rows, 0, pivots, groups)
    inverse_copy.wait()
    result[...] = dot3(split(columns), split(load[...]))
    result_copy = pltpu.make_async_copy(result, factor, sem.at[3])
    result_copy.start()
    codes, exponents = encode(result[...])
    later_codes, later_exponents = encode(later[...])
    kept, kept_later = rows - pivots, rows - dead
    code[:kept] = codes[pivots:]
    code[kept : kept + kept_later] = later_codes[dead:]
    row = lax.broadcasted_iota(jnp.int32, exponents.shape, 0)
    code[kept + kept_later :] = jnp.where(row == 0, exponents, later_exponents).astype(jnp.int16)
    list_blocks(marks, groups, start, order, column, head, follow)
    later_copy.wait()
    result_copy.wait()


def left_kernel(pivots, gathered, factor, second, inverse, factors, left, pivot_code, exponent, sem):
    groups, code_rows, _ = gathered.shape
    rows, panel = factor.shape
    copies = [
        pltpu.make_async_copy(gathered.at[:, pl.ds(0, pivots), :], pivot_code, sem.at[0]),
        pltpu.make_async_copy(
            gathered.at[:, pl.ds(code_rows - ROWTILE, ROWTILE), :], exponent, sem.at[1]
        ),
    ]
    for copy in copies:
        copy.start()
    factors[0, 0] = factor[...]
    for copy in copies:
        copy.wait()
    lane = lax.broadcasted_iota(jnp.int32, (ROWTILE, panel), 1)
    total = jnp.zeros((ROWTILE, panel), jnp.float32)
    for g in range(groups):
        scale = pltpu.roll(scale_of(exponent[g]), (g * pivots - pivots) % panel, 1)
        total = jnp.where((lane >= g * pivots) & (lane < (g + 1) * pivots), scale, total)
    scale = total[:1]
    pivot_rows = split_code(pivot_code[...].reshape(groups * pivots, panel))
    inverse_parts = split(inverse[0, 0])
    first = factor[pivots:]
    update = dot3(split(first), pivot_rows) * scale
    result = dot3(split(second[pivots:] - update), inverse_parts)
    factors[0, 1, :pivots] = jnp.zeros((pivots, panel), jnp.float32)
    factors[0, 1, pivots:] = result
    own = dot3(split(result[pivots:]), inverse_parts, NN)
    mixed = first[pivots:] - dot3(split(own * scale), pivot_rows, NN)
    for k, part in enumerate((mixed, own)):
        high, low = split(part)
        left[k, :, :panel] = high
        left[k, :, panel : 2 * panel] = high
        left[k, :, 2 * panel :] = low


def update_kernel(
    pivots, label, head, follow, left, code, front, first, middle, base, edge, open_, right, acc
):
    rows, panel = right.shape[1], code.shape[2]
    groups = head.shape[0]
    block_rows = rows // groups
    dead = 2 * pivots
    step = pl.program_id(0)

    @pl.when(step == 0)
    def _():
        right[...] = jnp.zeros(right.shape, jnp.bfloat16)

    for d in range(2):
        acc[d] = front[0, :, d * rows : d * rows + 2 * LANE].astype(jnp.float32)

        def add(slot, d=d):
            k = slot % 2
            r = label[k, slot // 2] // groups
            where = pl.ds(pl.multiple_of(r * block_rows, block_rows), block_rows)
            source = pl.ds(pl.multiple_of(k * block_rows, block_rows), block_rows)
            acc[d, where, :LANE] += first[slot // 2, source, :].astype(jnp.float32)
            acc[d, where, LANE:] += middle[slot].astype(jnp.float32)
            return follow[slot]

        lax.while_loop(lambda slot: slot >= 0, add, head[2 * step + d])

    kept = (rows - pivots, rows - dead)
    starts = (0, kept[0])
    sides = []
    for d in range(2):
        scale = scale_of(code[d, kept[0] + kept[1] :])
        columns = slice(d * rows + 2 * LANE, (d + 1) * rows)
        total = jnp.concatenate(
            [acc[d, dead:], front[0, dead:, columns].astype(jnp.float32)], axis=1
        )
        for k in range(2):
            high, low = split_code(code[d, starts[k] : starts[k] + kept[k]])
            right[k, rows - kept[k] :, :panel] = high
            right[k, rows - kept[k] :, panel : 2 * panel] = low
            right[k, rows - kept[k] :, 2 * panel :] = high
            total = total - dot_nt(left[k], right[k]) * scale[k : k + 1]
        open_[d] = total[:, 2 * LANE :]
        sides.append(total.astype(jnp.bfloat16))
    even, odd = sides
    base[0] = jnp.concatenate([even[:, dead:], odd[:, dead:]], axis=1)
    edge[0] = jnp.concatenate([even[:, 2 * LANE - dead : 2 * LANE], odd[:, dead : 2 * dead]], axis=1)


def finish_kernel(pivots, start, order, column, rest, edge, open_, base, out, acc, even, odd, sem):
    groups, step_rows, width = acc.shape
    block_rows = rest.shape[1]
    dead = 2 * pivots
    pair_width = base.shape[2] // (groups // 2)
    per = step_rows // block_rows
    step, steps = pl.program_id(0), pl.num_programs(0)
    row = step * per + groups - steps * per
    acc[...] = jnp.zeros(acc.shape, jnp.float32)
    for p in range(per):

        @pl.loop(start[row + p], start[row + p + 1])
        def _(i):
            block = rest[order[i]].astype(jnp.float32)
            acc[column[i], p * block_rows : (p + 1) * block_rows, :] += block

    def copies(at, m):
        here = pl.ds(pl.multiple_of(at * step_rows, ROWTILE), step_rows)
        first = m * pair_width + LANE
        last = (m + 1) * pair_width - width
        return (
            pltpu.make_async_copy(
                even.at[at, m], out.at[0, here, pl.ds(first, even.shape[3])], sem.at[at, m]
            ),
            pltpu.make_async_copy(
                odd.at[at, m], out.at[0, here, pl.ds(last, width)], sem.at[at, groups // 2 + m]
            ),
        )

    for m in range(groups // 2):
        low = (open_[2 * m] + acc[2 * m]).astype(jnp.bfloat16)
        even[step, m] = jnp.concatenate([edge[m, :, :dead], low, edge[m, :, dead:]], axis=1)
        odd[step, m] = (open_[2 * m + 1] + acc[2 * m + 1]).astype(jnp.bfloat16)
        for copy in copies(step, m):
            copy.start()

    @pl.when(step == steps - 1)
    def _():
        @pl.loop(0, steps)
        def _(at):
            for m in range(groups // 2):
                for copy in copies(at, m):
                    copy.wait()


def local(front_entries, child_blocks, dest_device, dest_tile, child_count, diag_inverse):
    grp_total = lax.axis_size("grp")
    device_total = grp_total * lax.axis_size("front")
    axes = ("front", "grp")
    slots, block_rows, block_cols = child_blocks.shape
    _, rows, width = front_entries.shape
    panel = diag_inverse.shape[2]
    pivots = panel // grp_total
    slot_count = 2 * device_total
    rest_cols = block_cols - 2 * LANE
    hbm = pl.BlockSpec(memory_space=pl.ANY)
    smem = pl.BlockSpec(memory_space=pltpu.SMEM)
    whole = lambda *shape: pl.BlockSpec(shape, lambda i: (0,) * len(shape))

    first_rows = 2 * block_rows + LABELROWS
    first_out, position = pl.pallas_call(
        pack_first_kernel,
        grid=(1,),
        out_shape=(
            jax.ShapeDtypeStruct((device_total, first_rows, LANE), jnp.bfloat16),
            jax.ShapeDtypeStruct((slots,), jnp.int32),
        ),
        in_specs=[smem, smem, smem, hbm],
        out_specs=(hbm, smem),
        scratch_shapes=[
            pltpu.VMEM((slots, block_rows, LANE), jnp.bfloat16),
            pltpu.VMEM((device_total + 1, first_rows, LANE), jnp.bfloat16),
            pltpu.SMEM((3, device_total), jnp.int32),
            pltpu.SemaphoreType.DMA,
        ],
        compiler_params=params(),
        name="pack_first",
    )(child_count, dest_device.reshape(slots), dest_tile, child_blocks)
    first = lax.all_to_all(first_out, axes, split_axis=0, concat_axis=0, tiled=True)
    middle_out, rest_out, entries = pl.pallas_call(
        pack_rest_kernel,
        grid=(1,),
        out_shape=(
            jax.ShapeDtypeStruct((slot_count, block_rows, LANE), jnp.bfloat16),
            jax.ShapeDtypeStruct((slot_count, block_rows, rest_cols), jnp.bfloat16),
            jax.ShapeDtypeStruct((grp_total, rows, LANE), jnp.bfloat16),
        ),
        in_specs=[smem, whole(*child_blocks.shape), hbm],
        out_specs=(
            whole(slot_count, block_rows, LANE),
            whole(slot_count, block_rows, rest_cols),
            whole(grp_total, rows, LANE),
        ),
        scratch_shapes=[pltpu.SemaphoreType.DMA((grp_total,))],
        compiler_params=params(),
        cost_estimate=pl.CostEstimate(flops=0, bytes_accessed=16 * 2**20, transcendentals=0),
        name="pack_rest",
    )(position, child_blocks, front_entries)
    middle = lax.all_to_all(middle_out, axes, split_axis=0, concat_axis=0, tiled=True)
    first, rest_out, entries = lax.optimization_barrier((first, rest_out, entries))

    kept = rows - 2 * pivots
    code_rows = (rows - pivots) + kept + ROWTILE
    inverse_spec = lambda k: pl.BlockSpec((1, 1, panel, panel), lambda i: (0, k, 0, 0))
    row_blocks = rows // block_rows
    lengths = (row_blocks + 1, slot_count, slot_count, row_blocks, slot_count)
    factor, second, code, label, start, order, column, head, follow = pl.pallas_call(
        functools.partial(panel_kernel, pivots),
        grid=(1,),
        out_shape=(
            jax.ShapeDtypeStruct((rows, panel), jnp.float32),
            jax.ShapeDtypeStruct((rows, panel), jnp.float32),
            jax.ShapeDtypeStruct((code_rows, panel), jnp.int16),
            jax.ShapeDtypeStruct((LABELROWS, LANE), jnp.int32),
            *(jax.ShapeDtypeStruct((length,), jnp.int32) for length in lengths),
        ),
        in_specs=[hbm, whole(*entries.shape), hbm],
        out_specs=(hbm, hbm, whole(code_rows, panel), whole(LABELROWS, LANE)) + (smem,) * 5,
        scratch_shapes=[
            pltpu.VMEM((device_total + 1, first_rows, LANE), jnp.bfloat16),
            pltpu.VMEM((grp_total, rows + block_rows, LANE), jnp.float32),
            pltpu.SMEM((LABELROWS, LANE), jnp.int32),
            pltpu.VMEM((panel, panel), jnp.float32),
            pltpu.VMEM((rows, panel), jnp.float32),
            pltpu.VMEM((rows, panel), jnp.float32),
            pltpu.SemaphoreType.DMA((5,)),
        ],
        compiler_params=params(),
        cost_estimate=pl.CostEstimate(flops=2 * 10**9, bytes_accessed=10 * 2**20, transcendentals=0),
        name="panels",
    )(first, entries, diag_inverse)
    gathered = lax.all_gather(code, "grp", axis=0, tiled=False)

    gathered, rest_out = lax.optimization_barrier((gathered, rest_out))
    rest = lax.all_to_all(rest_out, axes, split_axis=0, concat_axis=0, tiled=True)

    factors, left = pl.pallas_call(
        functools.partial(left_kernel, pivots),
        grid=(1,),
        out_shape=(
            jax.ShapeDtypeStruct((1, 2, rows, panel), jnp.float32),
            jax.ShapeDtypeStruct((2, kept, 3 * panel), jnp.bfloat16),
        ),
        in_specs=[hbm, whole(rows, panel), whole(rows, panel), inverse_spec(1)],
        out_specs=(whole(1, 2, rows, panel), whole(2, kept, 3 * panel)),
        scratch_shapes=[
            pltpu.VMEM((grp_total, pivots, panel), jnp.int16),
            pltpu.VMEM((grp_total, ROWTILE, panel), jnp.int16),
            pltpu.SemaphoreType.DMA((2,)),
        ],
        compiler_params=params(),
        cost_estimate=pl.CostEstimate(flops=4 * 10**9, bytes_accessed=8 * 2**20, transcendentals=0),
        name="left_factors",
    )(gathered, factor, second, diag_inverse)

    base, edge, open_ = pl.pallas_call(
        functools.partial(update_kernel, pivots),
        grid=(grp_total // 2,),
        out_shape=(
            jax.ShapeDtypeStruct((1, kept, grp_total * kept), jnp.bfloat16),
            jax.ShapeDtypeStruct((grp_total // 2, kept, LANE), jnp.bfloat16),
            jax.ShapeDtypeStruct((grp_total, kept, rest_cols), jnp.float32),
        ),
        in_specs=[
            smem,
            smem,
            smem,
            whole(2, kept, 3 * panel),
            pl.BlockSpec((2, code_rows, panel), lambda i: (i, 0, 0)),
            pl.BlockSpec((1, rows, 2 * rows), lambda i: (0, 0, i)),
            whole(*first.shape),
            whole(*middle.shape),
        ],
        out_specs=(
            pl.BlockSpec((1, kept, 2 * kept), lambda i: (0, 0, i)),
            pl.BlockSpec((1, kept, LANE), lambda i: (i, 0, 0)),
            pl.BlockSpec((2, kept, rest_cols), lambda i: (i, 0, 0)),
        ),
        scratch_shapes=[
            pltpu.VMEM((2, rows, 3 * panel), jnp.bfloat16),
            pltpu.VMEM((2, rows, 2 * LANE), jnp.float32),
        ],
        compiler_params=params(),
        cost_estimate=pl.CostEstimate(flops=20 * 10**9, bytes_accessed=40 * 2**20, transcendentals=0),
        name="update",
    )(label, head, follow, left, gathered, front_entries, first, middle)

    step_rows = kept // 2
    schur = pl.pallas_call(
        functools.partial(finish_kernel, pivots),
        grid=(kept // step_rows,),
        out_shape=jax.ShapeDtypeStruct((1, kept, grp_total * kept), jnp.bfloat16),
        in_specs=[
            smem,
            smem,
            smem,
            whole(*rest.shape),
            pl.BlockSpec((grp_total // 2, step_rows, LANE), lambda i: (0, i, 0)),
            pl.BlockSpec((grp_total, step_rows, rest_cols), lambda i: (0, i, 0)),
            hbm,
        ],
        out_specs=hbm,
        input_output_aliases={6: 0},
        scratch_shapes=[
            pltpu.VMEM((grp_total, step_rows, rest_cols), jnp.float32),
            pltpu.VMEM((2, grp_total // 2, step_rows, rest_cols + LANE), jnp.bfloat16),
            pltpu.VMEM((2, grp_total // 2, step_rows, rest_cols), jnp.bfloat16),
            pltpu.SemaphoreType.DMA((2, grp_total)),
        ],
        compiler_params=params(),
        cost_estimate=pl.CostEstimate(flops=10**7, bytes_accessed=30 * 2**20, transcendentals=0),
        name="finish",
    )(start, order, column, rest, edge, open_, base)
    return schur, factors


def solution(mesh):
    placed = (
        P("front", "grp", None),
        P(("front", "grp"), None, None),
        P(("front", "grp"), None),
        P(("front", "grp")),
        P(("front", "grp")),
        P("front", None, None, None),
    )
    return jax.shard_map(
        local,
        mesh=mesh,
        in_specs=placed,
        out_specs=(P("front", "grp", None), P("front", None, "grp", None)),
        check_vma=False,
    )
```

```python
import functools

import jax
import jax.numpy as jnp
from jax import lax
from jax.experimental import pallas as pl
from jax.experimental.pallas import tpu as pltpu
from jax.sharding import PartitionSpec as P

LANE = 128
ROWTILE = 16
LABELROWS = 8
MIB = 1024 * 1024
NT = (((1,), (1,)), ((), ()))
NN = (((1,), (0,)), ((), ()))


def params(mebibytes=56):
    return pltpu.CompilerParams(vmem_limit_bytes=mebibytes * MIB)


def split(x):
    high = x.astype(jnp.bfloat16)
    return high, (x - high.astype(jnp.float32)).astype(jnp.bfloat16)


def dot_nt(a, b, form=NT):
    return lax.dot_general(a, b, form, preferred_element_type=jnp.float32)


def dot3(a, b, form=NT):
    a_high, a_low = a
    b_high, b_low = b
    return dot_nt(a_high, b_high, form) + (
        dot_nt(a_high, b_low, form) + dot_nt(a_low, b_high, form)
    )


def split_code(code):
    return split(code.astype(jnp.int32).astype(jnp.float32))


def encode(x):
    rows = x.shape[0]
    largest = jnp.max(jnp.abs(x), axis=1, keepdims=True)
    exponent = jnp.ceil(jnp.log2(jnp.clip(largest, 1e-30, 1e38)))
    scaled = jnp.round(x * jnp.exp2(15.0 - exponent))
    code = jnp.clip(scaled, -32767.0, 32767.0).astype(jnp.int32).astype(jnp.int16)
    along = jnp.transpose(jnp.broadcast_to(exponent, (rows, LANE)))[:ROWTILE]
    return code, along.astype(jnp.int32)


def scale_of(exponent):
    return jnp.exp2(exponent.astype(jnp.int32).astype(jnp.float32) - 15.0)


def pack_first_kernel(count, target, tile, blocks, packed, position, load, out, marks, sem, out_sem):
    devices = packed.shape[0]
    slots, rows, _ = blocks.shape
    copy = pltpu.make_async_copy(blocks.at[:, :, pl.ds(0, LANE)], load, sem)
    copy.start()

    @pl.loop(0, devices, unroll=8)
    def _(t):
        marks[2, t] = 2 * t
        marks[0, t] = 0
        marks[1, t] = 0

    @pl.loop(0, slots, unroll=4)
    def _(i):
        t = target[i]
        at = marks[2, t]
        marks[2, t] = at + 1
        position[i] = at
        marks[at % 2, t] = jnp.where(i < count[0], tile[i] + 1, 0)

    row = lax.broadcasted_iota(jnp.int32, (LABELROWS, LANE), 0)

    @pl.loop(0, devices, unroll=8)
    def _(t):
        both = jnp.where(row == 0, marks[0, t], jnp.where(row == 1, marks[1, t], 0))
        out[t, 2 * rows :, :] = both.astype(jnp.float32).astype(jnp.bfloat16)

    copy.wait()

    @pl.loop(0, slots, unroll=4)
    def _(i):
        at = position[i]
        out[at // 2, pl.ds(pl.multiple_of((at % 2) * rows, rows), rows), :] = load[i]

    parts = out_sem.shape[0]
    pieces = [pl.ds(n * (devices // parts), devices // parts) for n in range(parts)]
    copies = [
        pltpu.make_async_copy(out.at[piece], packed.at[piece], out_sem.at[n])
        for n, piece in enumerate(pieces)
    ]
    for copy in copies:
        copy.start()
    for copy in copies:
        copy.wait()


def pack_rest_kernel(position, blocks, front, middle, rest, entries, sem):
    groups = entries.shape[0]
    width = front.shape[2] // groups

    def copy(c):
        return pltpu.make_async_copy(
            front.at[0, :, pl.ds(c * width, LANE)], entries.at[c], sem.at[c]
        )

    for c in range(groups):
        copy(c).start()

    @pl.loop(0, blocks.shape[0], unroll=2)
    def _(i):
        at = position[i]
        middle[at] = blocks[i, :, LANE : 2 * LANE]
        rest[at] = blocks[i, :, 2 * LANE :]

    for c in range(groups):
        copy(c).wait()


def gather_lanes(acc, rows, start, width, groups):
    per = LANE // width
    lane = lax.broadcasted_iota(jnp.int32, (rows, LANE), 1)
    out = []
    for tile in range(groups // per):
        total = None
        for k in range(per):
            piece = acc[tile * per + k, :rows]
            shift = (k * width - start) % LANE
            if shift:
                piece = pltpu.roll(piece, shift, 1)
            total = piece if total is None else jnp.where(lane >= k * width, piece, total)
        out.append(total)
    return jnp.concatenate(out, axis=1)


def place_blocks(label, groups, start, order, column):
    sources = label.shape[1]
    start[groups] = 0

    @pl.loop(0, groups, unroll=4)
    def _(r):
        start[groups] += start[r]
        start[r] = start[groups]

    @pl.loop(0, sources, unroll=2)
    def _(source):
        for k in range(2):
            at = label[k, source]

            @pl.when(at >= 0)
            def _():
                r = at // groups
                index = start[r] - 1
                start[r] = index
                order[index] = 2 * source + k
                column[index] = at % groups


def panel_kernel(
    pivots, sent, entries, inverse, factor, second, code, label, start, order, column, head, follow,
    arrived, acc, marks, load, later, result, sem,
):
    groups, rows, _ = entries.shape
    sources = sent.shape[0]
    block_rows = rows // groups
    dead = 2 * pivots
    sent_copy = pltpu.make_async_copy(sent, arrived.at[pl.ds(0, sources)], sem.at[4])
    sent_copy.start()
    inverse_copy = pltpu.make_async_copy(inverse.at[0, 0], load, sem.at[1])
    inverse_copy.start()
    acc[:, :rows] = entries[...].astype(jnp.float32)
    sent_copy.wait()

    shape = (sources, LABELROWS, LANE)
    own = lax.broadcasted_iota(jnp.int32, shape, 0) == lax.broadcasted_iota(jnp.int32, shape, 2)
    marked = arrived[:sources, 2 * block_rows :, :].astype(jnp.float32)
    label[...] = jnp.sum(jnp.where(own, marked, 0.0), axis=0).astype(jnp.int32) - 1
    copy = pltpu.make_async_copy(label, marks, sem.at[0])
    copy.start()
    copy.wait()

    @pl.loop(0, groups + 1)
    def _(r):
        start[r] = 0
        head[r] = -1

    @pl.loop(0, sources, unroll=4)
    def _(source):
        for k in range(2):
            at = marks[k, source]
            spare = at < 0
            at = jnp.where(spare, groups * groups, at)
            r, c = at // groups, at % groups
            chain = jnp.where(spare, groups, c)
            start[r] += 1
            follow[2 * source + k] = head[chain]
            head[chain] = 2 * source + k
            where = pl.ds(pl.multiple_of(r * block_rows, block_rows), block_rows)
            block = arrived[source, k * block_rows : (k + 1) * block_rows, :]
            acc[c, where, :] += block.astype(jnp.float32)

    later[...] = gather_lanes(acc, rows, pivots, pivots, groups)
    later_copy = pltpu.make_async_copy(later, second, sem.at[2])
    later_copy.start()
    columns = gather_lanes(acc, rows, 0, pivots, groups)
    inverse_copy.wait()
    result[...] = dot3(split(columns), split(load[...]))
    result_copy = pltpu.make_async_copy(result, factor, sem.at[3])
    result_copy.start()
    codes, exponents = encode(result[...])
    later_codes, later_exponents = encode(later[...])
    kept, kept_later = rows - pivots, rows - dead
    code[:kept] = codes[pivots:]
    code[kept : kept + kept_later] = later_codes[dead:]
    row = lax.broadcasted_iota(jnp.int32, exponents.shape, 0)
    code[kept + kept_later :] = jnp.where(row == 0, exponents, later_exponents).astype(jnp.int16)
    place_blocks(marks, groups, start, order, column)
    later_copy.wait()
    result_copy.wait()


def left_kernel(pivots, gathered, factor, second, inverse, factors, left, pivot_code, exponent, sem):
    groups, code_rows, _ = gathered.shape
    rows, panel = factor.shape
    copies = [
        pltpu.make_async_copy(gathered.at[:, pl.ds(0, pivots), :], pivot_code, sem.at[0]),
        pltpu.make_async_copy(
            gathered.at[:, pl.ds(code_rows - ROWTILE, ROWTILE), :], exponent, sem.at[1]
        ),
    ]
    for copy in copies:
        copy.start()
    factors[0, 0] = factor[...]
    for copy in copies:
        copy.wait()
    lane = lax.broadcasted_iota(jnp.int32, (ROWTILE, panel), 1)
    total = jnp.zeros((ROWTILE, panel), jnp.float32)
    for g in range(groups):
        scale = pltpu.roll(scale_of(exponent[g]), (g * pivots - pivots) % panel, 1)
        total = jnp.where((lane >= g * pivots) & (lane < (g + 1) * pivots), scale, total)
    scale = total[:1]
    pivot_rows = split_code(pivot_code[...].reshape(groups * pivots, panel))
    inverse_parts = split(inverse[0, 0])
    first = factor[pivots:]
    update = dot3(split(first), pivot_rows) * scale
    result = dot3(split(second[pivots:] - update), inverse_parts)
    factors[0, 1, :pivots] = jnp.zeros((pivots, panel), jnp.float32)
    factors[0, 1, pivots:] = result
    own = dot3(split(result[pivots:]), inverse_parts, NN)
    mixed = first[pivots:] - dot3(split(own * scale), pivot_rows, NN)
    for k, part in enumerate((mixed, own)):
        high, low = split(part)
        left[k, :, :panel] = high
        left[k, :, panel : 2 * panel] = high
        left[k, :, 2 * panel :] = low


def update_kernel(
    pivots, label, head, follow, left, code, front, first, middle, base, edge, open_, right, acc
):
    rows, panel = right.shape[1], code.shape[2]
    groups = head.shape[0] - 1
    block_rows = rows // groups
    dead = 2 * pivots
    step = pl.program_id(0)

    @pl.when(step == 0)
    def _():
        right[...] = jnp.zeros(right.shape, jnp.bfloat16)

    for d in range(2):
        acc[d] = front[0, :, d * rows : d * rows + 2 * LANE].astype(jnp.float32)

        def add(slot, d=d):
            k = slot % 2
            r = label[k, slot // 2] // groups
            where = pl.ds(pl.multiple_of(r * block_rows, block_rows), block_rows)
            source = pl.ds(pl.multiple_of(k * block_rows, block_rows), block_rows)
            acc[d, where, :LANE] += first[slot // 2, source, :].astype(jnp.float32)
            acc[d, where, LANE:] += middle[slot].astype(jnp.float32)
            return follow[slot]

        lax.while_loop(lambda slot: slot >= 0, add, head[2 * step + d])

    kept = (rows - pivots, rows - dead)
    starts = (0, kept[0])
    sides = []
    for d in range(2):
        scale = scale_of(code[d, kept[0] + kept[1] :])
        columns = slice(d * rows + 2 * LANE, (d + 1) * rows)
        total = jnp.concatenate(
            [acc[d, dead:], front[0, dead:, columns].astype(jnp.float32)], axis=1
        )
        for k in range(2):
            high, low = split_code(code[d, starts[k] : starts[k] + kept[k]])
            right[k, rows - kept[k] :, :panel] = high
            right[k, rows - kept[k] :, panel : 2 * panel] = low
            right[k, rows - kept[k] :, 2 * panel :] = high
            total = total - dot_nt(left[k], right[k]) * scale[k : k + 1]
        open_[d] = total[:, 2 * LANE :]
        sides.append(total.astype(jnp.bfloat16))
    even, odd = sides
    base[0] = jnp.concatenate([even[:, dead:], odd[:, dead:]], axis=1)
    edge[0] = jnp.concatenate([even[:, 2 * LANE - dead : 2 * LANE], odd[:, dead : 2 * dead]], axis=1)


def finish_kernel(pivots, start, order, column, rest, edge, open_, base, out, acc, even, odd, sem):
    groups, step_rows, width = acc.shape
    block_rows = rest.shape[1]
    dead = 2 * pivots
    pair_width = base.shape[2] // (groups // 2)
    per = step_rows // block_rows
    step, steps = pl.program_id(0), pl.num_programs(0)
    row = step * per + groups - steps * per
    acc[...] = jnp.zeros(acc.shape, jnp.float32)
    for p in range(per):

        @pl.loop(start[row + p], start[row + p + 1])
        def _(i):
            block = rest[order[i]].astype(jnp.float32)
            acc[column[i], p * block_rows : (p + 1) * block_rows, :] += block

    def copies(at, m):
        here = pl.ds(pl.multiple_of(at * step_rows, ROWTILE), step_rows)
        first = m * pair_width + LANE
        last = (m + 1) * pair_width - width
        return (
            pltpu.make_async_copy(
                even.at[at, m], out.at[0, here, pl.ds(first, even.shape[3])], sem.at[at, m]
            ),
            pltpu.make_async_copy(
                odd.at[at, m], out.at[0, here, pl.ds(last, width)], sem.at[at, groups // 2 + m]
            ),
        )

    for m in range(groups // 2):
        low = (open_[2 * m] + acc[2 * m]).astype(jnp.bfloat16)
        even[step, m] = jnp.concatenate([edge[m, :, :dead], low, edge[m, :, dead:]], axis=1)
        odd[step, m] = (open_[2 * m + 1] + acc[2 * m + 1]).astype(jnp.bfloat16)
        for copy in copies(step, m):
            copy.start()

    @pl.when(step == steps - 1)
    def _():
        @pl.loop(0, steps)
        def _(at):
            for m in range(groups // 2):
                for copy in copies(at, m):
                    copy.wait()


def local(front_entries, child_blocks, dest_device, dest_tile, child_count, diag_inverse):
    grp_total = lax.axis_size("grp")
    device_total = grp_total * lax.axis_size("front")
    axes = ("front", "grp")
    slots, block_rows, block_cols = child_blocks.shape
    _, rows, width = front_entries.shape
    panel = diag_inverse.shape[2]
    pivots = panel // grp_total
    slot_count = 2 * device_total
    rest_cols = block_cols - 2 * LANE
    hbm = pl.BlockSpec(memory_space=pl.ANY)
    smem = pl.BlockSpec(memory_space=pltpu.SMEM)
    whole = lambda *shape: pl.BlockSpec(shape, lambda i: (0,) * len(shape))

    first_rows = 2 * block_rows + LABELROWS
    first_out, position = pl.pallas_call(
        pack_first_kernel,
        grid=(1,),
        out_shape=(
            jax.ShapeDtypeStruct((device_total, first_rows, LANE), jnp.bfloat16),
            jax.ShapeDtypeStruct((slots,), jnp.int32),
        ),
        in_specs=[smem, smem, smem, hbm],
        out_specs=(hbm, smem),
        scratch_shapes=[
            pltpu.VMEM((slots, block_rows, LANE), jnp.bfloat16),
            pltpu.VMEM((device_total + 1, first_rows, LANE), jnp.bfloat16),
            pltpu.SMEM((3, device_total), jnp.int32),
            pltpu.SemaphoreType.DMA,
            pltpu.SemaphoreType.DMA((4,)),
        ],
        compiler_params=params(),
        name="pack_first",
    )(child_count, dest_device.reshape(slots), dest_tile, child_blocks)
    first = lax.all_to_all(first_out, axes, split_axis=0, concat_axis=0, tiled=True)
    middle_out, rest_out, entries = pl.pallas_call(
        pack_rest_kernel,
        grid=(1,),
        out_shape=(
            jax.ShapeDtypeStruct((slot_count, block_rows, LANE), jnp.bfloat16),
            jax.ShapeDtypeStruct((slot_count, block_rows, rest_cols), jnp.bfloat16),
            jax.ShapeDtypeStruct((grp_total, rows, LANE), jnp.bfloat16),
        ),
        in_specs=[smem, whole(*child_blocks.shape), hbm],
        out_specs=(
            whole(slot_count, block_rows, LANE),
            whole(slot_count, block_rows, rest_cols),
            whole(grp_total, rows, LANE),
        ),
        scratch_shapes=[pltpu.SemaphoreType.DMA((grp_total,))],
        compiler_params=params(),
        cost_estimate=pl.CostEstimate(flops=0, bytes_accessed=16 * 2**20, transcendentals=0),
        name="pack_rest",
    )(position, child_blocks, front_entries)
    middle = lax.all_to_all(middle_out, axes, split_axis=0, concat_axis=0, tiled=True)
    first, rest_out, entries = lax.optimization_barrier((first, rest_out, entries))

    kept = rows - 2 * pivots
    code_rows = (rows - pivots) + kept + ROWTILE
    inverse_spec = lambda k: pl.BlockSpec((1, 1, panel, panel), lambda i: (0, k, 0, 0))
    row_blocks = rows // block_rows
    lengths = (row_blocks + 1, slot_count, slot_count, row_blocks + 1, slot_count)
    factor, second, code, label, start, order, column, head, follow = pl.pallas_call(
        functools.partial(panel_kernel, pivots),
        grid=(1,),
        out_shape=(
            jax.ShapeDtypeStruct((rows, panel), jnp.float32),
            jax.ShapeDtypeStruct((rows, panel), jnp.float32),
            jax.ShapeDtypeStruct((code_rows, panel), jnp.int16),
            jax.ShapeDtypeStruct((LABELROWS, LANE), jnp.int32),
            *(jax.ShapeDtypeStruct((length,), jnp.int32) for length in lengths),
        ),
        in_specs=[hbm, whole(*entries.shape), hbm],
        out_specs=(hbm, hbm, whole(code_rows, panel), whole(LABELROWS, LANE)) + (smem,) * 5,
        scratch_shapes=[
            pltpu.VMEM((device_total + 1, first_rows, LANE), jnp.bfloat16),
            pltpu.VMEM((grp_total, rows + block_rows, LANE), jnp.float32),
            pltpu.SMEM((LABELROWS, LANE), jnp.int32),
            pltpu.VMEM((panel, panel), jnp.float32),
            pltpu.VMEM((rows, panel), jnp.float32),
            pltpu.VMEM((rows, panel), jnp.float32),
            pltpu.SemaphoreType.DMA((5,)),
        ],
        compiler_params=params(),
        cost_estimate=pl.CostEstimate(flops=2 * 10**9, bytes_accessed=10 * 2**20, transcendentals=0),
        name="panels",
    )(first, entries, diag_inverse)
    gathered = lax.all_gather(code, "grp", axis=0, tiled=False)

    gathered, rest_out = lax.optimization_barrier((gathered, rest_out))
    rest = lax.all_to_all(rest_out, axes, split_axis=0, concat_axis=0, tiled=True)

    factors, left = pl.pallas_call(
        functools.partial(left_kernel, pivots),
        grid=(1,),
        out_shape=(
            jax.ShapeDtypeStruct((1, 2, rows, panel), jnp.float32),
            jax.ShapeDtypeStruct((2, kept, 3 * panel), jnp.bfloat16),
        ),
        in_specs=[hbm, whole(rows, panel), whole(rows, panel), inverse_spec(1)],
        out_specs=(whole(1, 2, rows, panel), whole(2, kept, 3 * panel)),
        scratch_shapes=[
            pltpu.VMEM((grp_total, pivots, panel), jnp.int16),
            pltpu.VMEM((grp_total, ROWTILE, panel), jnp.int16),
            pltpu.SemaphoreType.DMA((2,)),
        ],
        compiler_params=params(),
        cost_estimate=pl.CostEstimate(flops=4 * 10**9, bytes_accessed=8 * 2**20, transcendentals=0),
        name="left_factors",
    )(gathered, factor, second, diag_inverse)

    base, edge, open_ = pl.pallas_call(
        functools.partial(update_kernel, pivots),
        grid=(grp_total // 2,),
        out_shape=(
            jax.ShapeDtypeStruct((1, kept, grp_total * kept), jnp.bfloat16),
            jax.ShapeDtypeStruct((grp_total // 2, kept, LANE), jnp.bfloat16),
            jax.ShapeDtypeStruct((grp_total, kept, rest_cols), jnp.float32),
        ),
        in_specs=[
            smem,
            smem,
            smem,
            whole(2, kept, 3 * panel),
            pl.BlockSpec((2, code_rows, panel), lambda i: (i, 0, 0)),
            pl.BlockSpec((1, rows, 2 * rows), lambda i: (0, 0, i)),
            whole(*first.shape),
            whole(*middle.shape),
        ],
        out_specs=(
            pl.BlockSpec((1, kept, 2 * kept), lambda i: (0, 0, i)),
            pl.BlockSpec((1, kept, LANE), lambda i: (i, 0, 0)),
            pl.BlockSpec((2, kept, rest_cols), lambda i: (i, 0, 0)),
        ),
        scratch_shapes=[
            pltpu.VMEM((2, rows, 3 * panel), jnp.bfloat16),
            pltpu.VMEM((2, rows, 2 * LANE), jnp.float32),
        ],
        compiler_params=params(),
        cost_estimate=pl.CostEstimate(flops=20 * 10**9, bytes_accessed=40 * 2**20, transcendentals=0),
        name="update",
    )(label, head, follow, left, gathered, front_entries, first, middle)

    step_rows = kept // 2
    schur = pl.pallas_call(
        functools.partial(finish_kernel, pivots),
        grid=(kept // step_rows,),
        out_shape=jax.ShapeDtypeStruct((1, kept, grp_total * kept), jnp.bfloat16),
        in_specs=[
            smem,
            smem,
            smem,
            whole(*rest.shape),
            pl.BlockSpec((grp_total // 2, step_rows, LANE), lambda i: (0, i, 0)),
            pl.BlockSpec((grp_total, step_rows, rest_cols), lambda i: (0, i, 0)),
            hbm,
        ],
        out_specs=hbm,
        input_output_aliases={6: 0},
        scratch_shapes=[
            pltpu.VMEM((grp_total, step_rows, rest_cols), jnp.float32),
            pltpu.VMEM((2, grp_total // 2, step_rows, rest_cols + LANE), jnp.bfloat16),
            pltpu.VMEM((2, grp_total // 2, step_rows, rest_cols), jnp.bfloat16),
            pltpu.SemaphoreType.DMA((2, grp_total)),
        ],
        compiler_params=params(),
        cost_estimate=pl.CostEstimate(flops=10**7, bytes_accessed=30 * 2**20, transcendentals=0),
        name="finish",
    )(start, order, column, rest, edge, open_, base)
    return schur, factors


def solution(mesh):
    placed = (
        P("front", "grp", None),
        P(("front", "grp"), None, None),
        P(("front", "grp"), None),
        P(("front", "grp")),
        P(("front", "grp")),
        P("front", None, None, None),
    )
    return jax.shard_map(
        local,
        mesh=mesh,
        in_specs=placed,
        out_specs=(P("front", "grp", None), P("front", None, "grp", None)),
        check_vma=False,
    )
```
